32 devices in a mesh: teacher: 4 (over x, core), vocab: 8 (over z, y).
Axes of the slice: x: 2, y: 2, z: 4, core: 2. Of those that a mesh axis runs over, the one named last changes fastest.
Arguments:
- teacher_hidden: bfloat16 [4, 128, 2048], P('teacher', 'vocab'), may hold values from -32 to 32
- teacher_head: bfloat16 [2048, 16384], P('teacher', 'vocab'), may hold values from -1 to 1
- student_hidden: bfloat16 [128, 2048], P(None, 'teacher'), may hold values from -32 to 32
- student_head: bfloat16 [2048, 16384], P('teacher', 'vocab'), may hold values from -1 to 1
- labels: int32 [128], P('teacher'), may hold values from 0 to 16383
Outputs:
- ce_matrix: float32 [128, 4, 4], P('teacher')
- agreement: float32 [128, 4], P('teacher')
- student_grad: float32 [2048, 16384], P('teacher', 'vocab')
The draws below stay inside these ranges and needn't reach their ends.
All inputs are finite; a program needn't handle non-finite values.
Results may differ from the reference program's by a relative error of at most 0.0065.
Values may be sent and summed in bfloat16 or wider, within the bound.
No kernel may reach another device: no remote copies, remote signals or barrier semaphores. Data moves between devices by JAX's collectives and lax.ppermute only.
A program may use at most 64 MiB of HBM per device.

```python
import math
import jax
import jax.numpy as jnp
from jax import lax

D = 2048
TOKENS = 128
TEACHERS = 4
VOCAB = 16384


def head_columns(key, stream, chosen_cols):
    head_key = jax.random.fold_in(key, stream)

    def one_column(column):
        return jax.random.normal(jax.random.fold_in(head_key, column), (D,), jnp.float32)
    values = jax.vmap(one_column)(chosen_cols)
    return jnp.clip(values * (3.0 / math.sqrt(D)), -1.0, 1.0)


def draw_head(key, stream):
    return head_columns(key, stream, jnp.arange(VOCAB, dtype=jnp.int32)).T.astype(jnp.bfloat16)


def strength_levels():
    levels = jnp.array([30.0, 45.0, 60.0], jnp.float32)
    return levels


def peak_rows(key, stream, first_cols, second_cols, first_logit, second_logit):
    first_vecs = head_columns(key, stream, first_cols)
    second_vecs = head_columns(key, stream, second_cols)
    first_square = jnp.sum(first_vecs * first_vecs, axis=1, keepdims=True)
    cross_dot = jnp.sum(first_vecs * second_vecs, axis=1, keepdims=True)
    along_ratio = cross_dot / first_square
    normal_part = second_vecs - along_ratio * first_vecs
    normal_square = jnp.sum(normal_part * normal_part, axis=1, keepdims=True)
    along_second = second_logit[:, None] - along_ratio * first_logit[:, None]
    peaked = first_logit[:, None] * first_vecs / first_square + along_second * normal_part / normal_square
    return jnp.clip(peaked, -32.0, 32.0)


def column_pair(key, stream, count):
    first_cols = jax.random.randint(jax.random.fold_in(key, stream), (count,), 0, VOCAB)
    offsets = jax.random.randint(jax.random.fold_in(key, stream + 1), (count,), 1, VOCAB)
    return (first_cols, (first_cols + offsets) % VOCAB)


def scaled_rows(key, plain_rows):
    result = plain_rows
    return result


def draw_teacher_head(key, part):
    return draw_head(key, 10)


def draw_student_head(key, part):
    return draw_head(key, 20)


def draw_teacher_hidden(key, part):
    plain_rows = jnp.clip(jax.random.normal(jax.random.fold_in(key, 11), (TEACHERS, TOKENS, D), jnp.float32), -6.0, 6.0)
    plain_rows = scaled_rows(key, plain_rows)
    marked_count = TOKENS // 4
    marked_ids = 4 * jnp.arange(marked_count, dtype=jnp.int32) + 1
    first_cols, second_cols = column_pair(key, 14, marked_count)
    level_pick = jax.random.randint(jax.random.fold_in(key, 16), (TEACHERS, marked_count), 0, 3)
    leading = jax.random.randint(jax.random.fold_in(key, 17), (TEACHERS, marked_count), 0, 2).astype(jnp.float32)
    top_logit = strength_levels()[level_pick]
    first_logit = (top_logit - 2.0 * (1.0 - leading)).reshape(-1)
    second_logit = (top_logit - 2.0 * leading).reshape(-1)
    first_all = jnp.broadcast_to(first_cols[None, :], (TEACHERS, marked_count)).reshape(-1)
    second_all = jnp.broadcast_to(second_cols[None, :], (TEACHERS, marked_count)).reshape(-1)
    peaked = peak_rows(key, 10, first_all, second_all, first_logit, second_logit).reshape(TEACHERS, marked_count, D)
    result = plain_rows.at[:, marked_ids, :].set(peaked)
    return result.astype(jnp.bfloat16)


def draw_student_hidden(key, part):
    shared = jnp.clip(jax.random.normal(jax.random.fold_in(key, 21), (1, D), jnp.float32), -4.0, 4.0)
    noise_rows = jnp.clip(jax.random.normal(jax.random.fold_in(key, 22), (TOKENS, D), jnp.float32), -4.0, 4.0)
    plain_rows = 0.2 * (shared + noise_rows)
    plain_rows = scaled_rows(key, plain_rows)
    first_cols, second_cols = column_pair(key, 24, TOKENS)
    level_pick = jax.random.randint(jax.random.fold_in(key, 26), (TOKENS,), 0, 3)
    top_logit = strength_levels()[level_pick]
    peaked = peak_rows(key, 20, first_cols, second_cols, top_logit, top_logit - 2.0)
    marked = jnp.arange(TOKENS, dtype=jnp.int32) % 16 == 6
    result = jnp.where(marked[:, None], peaked, plain_rows)
    return result.astype(jnp.bfloat16)


def set_ends(values, rng, least, top_value):
    extent = values.shape
    place = [jax.random.randint(jax.random.fold_in(rng, axis), (), 0, extent[axis]) for axis in range(len(extent))]
    values = values.at[tuple(place)].set(least)
    longest = extent.index(max(extent))
    place[longest] = (place[longest] + 1) % extent[longest]
    return values.at[tuple(place)].set(top_value)


def setup_inputs(seed: int = 0) -> dict:
    key_of = jax.random.split(jax.random.key(seed), 6)
    return {
        "teacher_hidden": draw_teacher_hidden(jax.random.fold_in(key_of[5], 71), 0),
        "teacher_head": draw_teacher_head(jax.random.fold_in(key_of[5], 71), 0),
        "student_hidden": draw_student_hidden(jax.random.fold_in(key_of[5], 71), 0),
        "student_head": draw_student_head(jax.random.fold_in(key_of[5], 71), 0),
        "labels": set_ends(jax.random.randint(key_of[4], (TOKENS,), 0, VOCAB), jax.random.fold_in(key_of[4], 1), 0, VOCAB - 1).astype(jnp.int32),
    }


HARD_SHARE = 0.3


def log_softmax(logits):
    highest = jnp.max(logits, axis=1, keepdims=True)
    summed = jnp.sum(jnp.exp(logits - highest), axis=1, keepdims=True)
    return logits - (highest + jnp.log(summed))


def reference(teacher_hidden, teacher_head, student_hidden, student_head, labels):
    def teacher_rows(hidden):
        logits = jnp.dot(hidden, teacher_head, preferred_element_type=jnp.float32)
        return log_softmax(logits).astype(jnp.bfloat16)

    log_probs = lax.map(teacher_rows, teacher_hidden)
    teacher_prob = jnp.exp(log_probs.astype(jnp.float32)).astype(jnp.bfloat16)
    block_rows = TOKENS // TEACHERS
    columns = jnp.arange(VOCAB, dtype=jnp.int32)

    def block_terms(block_index):
        offset = (block_index * block_rows).astype(jnp.int32)
        prob_block = lax.dynamic_slice_in_dim(teacher_prob, offset, block_rows, 1).astype(jnp.float32)
        logprob_block = lax.dynamic_slice_in_dim(log_probs, offset, block_rows, 1).astype(jnp.float32)
        cross_block = -jnp.einsum("itv,jtv->tij", prob_block, logprob_block)
        disagree = jnp.mean(cross_block, axis=1)
        inverse = 1.0 / (1.0 + disagree)
        weights = inverse / jnp.sum(inverse, axis=1, keepdims=True)
        soft_mix = jnp.einsum("ti,itv->tv", weights, prob_block)
        label_block = lax.dynamic_slice_in_dim(labels, offset, block_rows, 0)
        onehot = (columns[None, :] == label_block[:, None]).astype(jnp.float32)
        target = (1.0 - HARD_SHARE) * soft_mix + HARD_SHARE * onehot
        hidden_block = lax.dynamic_slice_in_dim(student_hidden, offset, block_rows, 0)
        student_logits = jnp.dot(hidden_block, student_head, preferred_element_type=jnp.float32)
        student_prob = jnp.exp(log_softmax(student_logits))
        residual = (student_prob - target).astype(jnp.bfloat16)
        return cross_block, weights * TEACHERS, residual

    cross_all, agreement, residual = lax.map(block_terms, jnp.arange(TEACHERS, dtype=jnp.int32))
    cross_all = cross_all.reshape(TOKENS, TEACHERS, TEACHERS)
    agreement = agreement.reshape(TOKENS, TEACHERS)
    residual = residual.reshape(TOKENS, VOCAB)
    student_grad = lax.dot_general(student_hidden, residual, (((0,), (0,)), ((), ())), preferred_element_type=jnp.float32)
    return (cross_all, agreement, student_grad)
```

```python
import functools

import jax
import jax.numpy as jnp
from jax import lax
from jax.experimental import pallas as pl
from jax.experimental.pallas import tpu as pltpu
from jax.sharding import PartitionSpec as P

HARD_SHARE = 0.3
LANES = 128


def swap(value, axis, mask):
    count = lax.axis_size(axis)
    return lax.ppermute(value, axis, [(i, i ^ mask) for i in range(count)])


def call(body, outs, args, grid=None, in_specs=None, out_specs=None, scratch=(), flops=0, moved=0):
    extra = {} if grid is None else {"grid": grid}
    if in_specs is not None:
        extra["in_specs"] = in_specs
    if out_specs is not None:
        extra["out_specs"] = out_specs
    return pl.pallas_call(
        body,
        out_shape=outs,
        scratch_shapes=list(scratch),
        compiler_params=pltpu.CompilerParams(vmem_limit_bytes=48 * 1024 * 1024),
        cost_estimate=pl.CostEstimate(flops=flops, bytes_accessed=moved, transcendentals=0),
        **extra,
    )(*args)


def partial_body(hidden_ref, own_ref, sib_ref, out_ref):
    half = own_ref.shape[0]
    out_ref[...] = jnp.dot(
        hidden_ref[:, :half], own_ref[...], preferred_element_type=jnp.float32
    ) + jnp.dot(hidden_ref[:, half:], sib_ref[...], preferred_element_type=jnp.float32)


def stats_body(kept_ref, came_ref, student_ref, logits_ref, lse_ref, mean_ref):
    teachers, rows, _ = kept_ref.shape
    lane = lax.broadcasted_iota(jnp.int32, (rows, LANES), 1)
    lse = jnp.zeros((rows, LANES), jnp.float32)
    mean = jnp.zeros((rows, LANES), jnp.float32)
    tops = []
    for i in range(teachers):
        value = kept_ref[i] + came_ref[i].astype(jnp.float32)
        logits_ref[i] = value
        tops.append(jnp.max(value, axis=1, keepdims=True))
    for i in range(teachers):
        weight = jnp.exp(logits_ref[i] - tops[i])
        total = jnp.sum(weight, axis=1, keepdims=True)
        group = (lane >= i * teachers) & (lane < (i + 1) * teachers)
        lse = jnp.where(group, tops[i] + jnp.log(total), lse)
        for j in range(teachers):
            local = jnp.sum(weight * (logits_ref[j] - tops[j]), axis=1, keepdims=True) / total + tops[j]
            mean = jnp.where(lane == i * teachers + j, local, mean)
    value = student_ref[...]
    top = jnp.max(value, axis=1, keepdims=True)
    total = jnp.sum(jnp.exp(value - top), axis=1, keepdims=True)
    lse_ref[...] = jnp.where(lane == teachers * teachers, top + jnp.log(total), lse)
    mean_ref[...] = mean


def merge(lse, mean, other_lse, other_mean):
    high = jnp.maximum(lse, other_lse)
    low = jnp.minimum(lse, other_lse)
    both = high + jnp.log1p(jnp.exp(low - high))
    return both, jnp.exp(lse - both) * mean + jnp.exp(other_lse - both) * other_mean


def residual_body(logits_ref, student_ref, lse_ref, mean_ref, label_ref, cross_ref, agree_ref, residual_ref):
    teachers, rows, width = logits_ref.shape
    lane = lax.broadcasted_iota(jnp.int32, (rows, LANES), 1)
    lse, mean = lse_ref[...], mean_ref[...]
    norms = [lse[:, i * teachers : i * teachers + 1] for i in range(teachers)]
    cross = jnp.zeros((rows, LANES), jnp.float32)
    inverse = []
    for j in range(teachers):
        spread = jnp.zeros((rows, 1), jnp.float32)
        for i in range(teachers):
            at = i * teachers + j
            entry = norms[j] - mean[:, at : at + 1]
            cross = jnp.where(lane == at, entry, cross)
            spread = spread + entry
        inverse.append(1.0 / (1.0 + spread * (1.0 / teachers)))
    cross_ref[...] = cross
    total = inverse[0]
    for i in range(1, teachers):
        total = total + inverse[i]
    weights = [value / total for value in inverse]
    agree = jnp.zeros((rows, LANES), jnp.float32)
    for i in range(teachers):
        agree = jnp.where(lane == i, weights[i] * teachers, agree)
    agree_ref[...] = agree
    at = teachers * teachers
    target = jnp.where(
        lax.broadcasted_iota(jnp.int32, (rows, width), 1) == label_ref[...], HARD_SHARE, 0.0
    )
    for i in range(teachers):
        log_prob = (logits_ref[i] - norms[i]).astype(jnp.bfloat16).astype(jnp.float32)
        prob = jnp.exp(log_prob).astype(jnp.bfloat16).astype(jnp.float32)
        target = target + ((1.0 - HARD_SHARE) * weights[i]) * prob
    prob = jnp.exp(student_ref[...] - lse[:, at : at + 1])
    residual_ref[...] = (prob - target).astype(jnp.bfloat16)


def grad_body(hidden_ref, residual_ref, out_ref):
    out_ref[...] = jnp.dot(hidden_ref[...], residual_ref[...], preferred_element_type=jnp.float32)


def fast(teacher_hidden, teacher_head, student_hidden, student_head, labels):
    teachers = lax.axis_size("teacher")
    shards = lax.axis_size("vocab")
    chips = teachers // 2
    rows, width = teacher_head.shape
    tokens = student_hidden.shape[0]
    piece = tokens // shards // 2
    block = tokens // teachers
    x = lax.axis_index("teacher") // 2
    core = lax.axis_index("teacher") % 2
    f32 = jnp.float32

    sib_head = swap(teacher_head, "teacher", 1)
    sib_labels = swap(labels, "teacher", 1)

    ordered = student_hidden.reshape(chips, shards // chips, 2, piece, rows).transpose(0, 2, 1, 3, 4)
    ordered = ordered.reshape(tokens, rows)
    student = lax.psum_scatter(
        jnp.dot(ordered, student_head, preferred_element_type=f32), "teacher", scatter_dimension=0, tiled=True
    )
    ordered_t = ordered.T

    mine = teacher_hidden[0].reshape(2, piece, chips, 2, rows)
    parts = []
    for to in range(teachers):
        half = mine[to % 2, :, to // 2]
        parts.append(jnp.concatenate([half[:, to % 2], half[:, 1 - to % 2]], axis=1))
    spread = jnp.broadcast_to(jnp.stack(parts)[:, None], (teachers, shards, piece, 2 * rows))
    spread = spread.reshape(teachers * shards, piece, 2 * rows)
    came = lax.all_to_all(spread, ("teacher", "vocab"), 0, 0, tiled=True)
    came = came.reshape(teachers * shards * piece, 2 * rows)

    step = min(width, 512)
    partial = call(
        partial_body,
        jax.ShapeDtypeStruct((came.shape[0], width), f32),
        (came, teacher_head, sib_head),
        grid=(width // step,),
        in_specs=[
            pl.BlockSpec(came.shape, lambda i: (0, 0)),
            pl.BlockSpec((rows, step), lambda i: (0, i)),
            pl.BlockSpec((rows, step), lambda i: (0, i)),
        ],
        out_specs=pl.BlockSpec((came.shape[0], step), lambda i: (0, i)),
        flops=2 * came.shape[0] * 2 * rows * width,
        moved=4 * rows * width,
    )
    partial = partial.reshape(teachers, chips, block, width)
    kept = lax.dynamic_index_in_dim(partial, x, 1, keepdims=False)
    sent = lax.dynamic_index_in_dim(partial, 1 - x, 1, keepdims=False).astype(jnp.float16)
    other = swap(sent, "teacher", 2).astype(f32)

    flat = jax.ShapeDtypeStruct((block, LANES), f32)
    logits, lse, mean = call(
        stats_body,
        (jax.ShapeDtypeStruct((teachers, block, width), f32), flat, flat),
        (kept, other, student),
    )
    mask = 1
    while mask < shards:
        both = swap(jnp.stack([lse, mean]), "vocab", mask)
        lse, mean = merge(lse, mean, both[0], both[1])
        mask *= 2

    pair = jnp.where(core == 0, jnp.stack([labels, sib_labels]), jnp.stack([sib_labels, labels]))
    chosen = lax.dynamic_index_in_dim(
        pair.reshape(shards // chips, 2, piece), core, 1, keepdims=False
    ).reshape(block, 1)
    local_label = chosen - lax.axis_index("vocab") * width
    cross, agree, residual = call(
        residual_body,
        (flat, flat, jax.ShapeDtypeStruct((block, width), jnp.bfloat16)),
        (logits, student, lse, mean, local_label),
    )
    gathered = lax.all_gather(residual, "teacher", axis=0, tiled=True)
    grad = call(
        grad_body,
        jax.ShapeDtypeStruct((rows, width), f32),
        (ordered_t, gathered),
        grid=(width // step,),
        in_specs=[
            pl.BlockSpec((rows, tokens), lambda i: (0, 0)),
            pl.BlockSpec((tokens, step), lambda i: (0, i)),
        ],
        out_specs=pl.BlockSpec((rows, step), lambda i: (0, i)),
        flops=2 * rows * tokens * width,
        moved=4 * rows * width,
    )

    small = jnp.concatenate([cross[:, : teachers * teachers], agree[:, :teachers]], axis=1)
    sib_small = swap(small, "teacher", 1)
    lead = jnp.where(core == 0, small, sib_small).reshape(2, shards // chips // 2, piece, -1)
    trail = jnp.where(core == 0, sib_small, small).reshape(2, shards // chips // 2, piece, -1)
    lead = lax.dynamic_index_in_dim(lead, core, 0, keepdims=False)
    trail = lax.dynamic_index_in_dim(trail, core, 0, keepdims=False)
    small = jnp.stack([lead, trail], axis=1).reshape(block, -1)
    cross = small[:, : teachers * teachers].reshape(block, teachers, teachers)
    return cross, small[:, teachers * teachers :], grad


def normalizer(logits):
    highest = lax.pmax(jnp.max(logits, axis=1), "vocab")
    summed = lax.psum(jnp.sum(jnp.exp(logits - highest[:, None]), axis=1), "vocab")
    return highest + jnp.log(summed)


def general(teacher_hidden, teacher_head, student_hidden, student_head, labels):
    teachers = lax.axis_size("teacher")
    block_rows = student_hidden.shape[0] // teachers
    shard_width = teacher_head.shape[1]
    gathered = lax.all_gather(teacher_hidden, "vocab", axis=1, tiled=True)
    logits = jnp.dot(
        gathered[0],
        lax.all_gather(teacher_head, "teacher", axis=0, tiled=True),
        preferred_element_type=jnp.float32,
    )
    log_prob = (logits - normalizer(logits)[:, None]).astype(jnp.bfloat16)
    exchanged = lax.all_to_all(log_prob[None], "teacher", split_axis=1, concat_axis=0, tiled=True)
    teacher_prob = jnp.exp(exchanged.astype(jnp.float32)).astype(jnp.bfloat16)
    cross_local = -jnp.einsum("itv,jtv->tij", teacher_prob, exchanged, preferred_element_type=jnp.float32)
    cross_matrix = lax.psum(cross_local, "vocab")
    inverse = 1.0 / (1.0 + jnp.mean(cross_matrix, axis=1))
    weights = inverse / jnp.sum(inverse, axis=1, keepdims=True)
    soft_mix = jnp.sum(weights.T[:, :, None] * teacher_prob.astype(jnp.float32), axis=0)
    col_offset = lax.axis_index("vocab") * shard_width
    columns = lax.broadcasted_iota(jnp.int32, (block_rows, shard_width), 1) + col_offset
    onehot = (columns == labels[:, None]).astype(jnp.float32)
    target = (1.0 - HARD_SHARE) * soft_mix + HARD_SHARE * onehot
    student_logits = lax.psum_scatter(
        jnp.dot(student_hidden, student_head, preferred_element_type=jnp.float32),
        "teacher",
        scatter_dimension=0,
        tiled=True,
    )
    student_prob = jnp.exp(student_logits - normalizer(student_logits)[:, None])
    residual = (student_prob - target).astype(jnp.bfloat16)
    student_grad = lax.dot_general(
        student_hidden,
        lax.all_gather(residual, "teacher", axis=0, tiled=True),
        (((0,), (0,)), ((), ())),
        preferred_element_type=jnp.float32,
    )
    return (cross_matrix, weights * teachers, student_grad)


def solution(mesh):
    body = fast if mesh.shape["teacher"] == 4 and mesh.shape["vocab"] == 8 else general
    return jax.shard_map(
        body,
        mesh=mesh,
        in_specs=(
            P("teacher", "vocab", None),
            P("teacher", "vocab"),
            P(None, "teacher"),
            P("teacher", "vocab"),
            P("teacher"),
        ),
        out_specs=(P("teacher", None, None), P("teacher", None), P("teacher", "vocab")),
        check_vma=False,
    )
```

```python
import functools

import jax
import jax.numpy as jnp
from jax import lax
from jax.experimental import pallas as pl
from jax.experimental.pallas import tpu as pltpu
from jax.sharding import PartitionSpec as P

HARD_SHARE = 0.3
LANES = 128


def swap(value, axis, mask):
    count = lax.axis_size(axis)
    return lax.ppermute(value, axis, [(i, i ^ mask) for i in range(count)])


def call(body, outs, args, grid=None, in_specs=None, out_specs=None, scratch=(), flops=0, moved=0):
    extra = {} if grid is None else {"grid": grid}
    if in_specs is not None:
        extra["in_specs"] = in_specs
    if out_specs is not None:
        extra["out_specs"] = out_specs
    return pl.pallas_call(
        body,
        out_shape=outs,
        scratch_shapes=list(scratch),
        compiler_params=pltpu.CompilerParams(vmem_limit_bytes=16 * 1024 * 1024),
        cost_estimate=pl.CostEstimate(flops=flops, bytes_accessed=moved, transcendentals=0),
        **extra,
    )(*args)


VMEM = pl.BlockSpec(memory_space=pltpu.VMEM)
SMEM = pl.BlockSpec(memory_space=pltpu.SMEM)


def partial_body(step, which_ref, hidden_ref, own_ref, sib_ref, out_ref):
    teachers, _, block, depth = hidden_ref.shape
    half = depth // 2
    which = which_ref[0]
    rows = jnp.concatenate([hidden_ref[i, which] for i in range(teachers)], axis=0)

    @pl.loop(0, own_ref.shape[1] // step)
    def _(at):
        columns = pl.ds(pl.multiple_of(at * step, step), step)
        value = jnp.dot(rows[:, :half], own_ref[:, columns], preferred_element_type=jnp.float32)
        value += jnp.dot(rows[:, half:], sib_ref[:, columns], preferred_element_type=jnp.float32)
        for i in range(teachers):
            out_ref[i, :, columns] = value[i * block : (i + 1) * block]


def stats_body(kept_ref, came_ref, student_ref, logits_ref, stats_ref):
    teachers, rows, _ = kept_ref.shape
    lane = lax.broadcasted_iota(jnp.int32, (rows, LANES), 1)
    lse = jnp.zeros((rows, LANES), jnp.float32)
    mean = jnp.zeros((rows, LANES), jnp.float32)
    tops = []
    for i in range(teachers):
        value = kept_ref[i] + came_ref[i]
        logits_ref[i] = value
        tops.append(jnp.max(value, axis=1, keepdims=True))
    for i in range(teachers):
        weight = jnp.exp(logits_ref[i] - tops[i])
        total = jnp.sum(weight, axis=1, keepdims=True)
        group = (lane >= i * teachers) & (lane < (i + 1) * teachers)
        lse = jnp.where(group, tops[i] + jnp.log(total), lse)
        for j in range(teachers):
            local = jnp.sum(weight * (logits_ref[j] - tops[j]), axis=1, keepdims=True) / total + tops[j]
            mean = jnp.where(lane == i * teachers + j, local, mean)
    value = student_ref[...]
    top = jnp.max(value, axis=1, keepdims=True)
    total = jnp.sum(jnp.exp(value - top), axis=1, keepdims=True)
    stats_ref[0] = jnp.where(lane == teachers * teachers, top + jnp.log(total), lse)
    stats_ref[1] = mean


def merge(one, two):
    high = jnp.maximum(one[0], two[0])
    low = jnp.minimum(one[0], two[0])
    both = high + jnp.log1p(jnp.exp(low - high))
    return jnp.stack([both, jnp.exp(one[0] - both) * one[1] + jnp.exp(two[0] - both) * two[1]])


def residual_body(logits_ref, student_ref, stats_ref, label_ref, small_ref, residual_ref):
    teachers, rows, width = logits_ref.shape
    lane = lax.broadcasted_iota(jnp.int32, (rows, LANES), 1)
    lse, mean = stats_ref[0], stats_ref[1]
    norms = [lse[:, i * teachers : i * teachers + 1] for i in range(teachers)]
    small = jnp.zeros((rows, LANES), jnp.float32)
    inverse = []
    for j in range(teachers):
        spread = jnp.zeros((rows, 1), jnp.float32)
        for i in range(teachers):
            at = i * teachers + j
            entry = norms[j] - mean[:, at : at + 1]
            small = jnp.where(lane == at, entry, small)
            spread = spread + entry
        inverse.append(1.0 / (1.0 + spread * (1.0 / teachers)))
    total = inverse[0]
    for i in range(1, teachers):
        total = total + inverse[i]
    weights = [value / total for value in inverse]
    at = teachers * teachers
    for i in range(teachers):
        small = jnp.where(lane == at + i, weights[i] * teachers, small)
    square = jnp.concatenate([small, jnp.zeros((LANES - rows, LANES), jnp.float32)], axis=0)
    small_ref[...] = square.T[: small_ref.shape[0]]
    target = jnp.where(
        lax.broadcasted_iota(jnp.int32, (rows, width), 1) == label_ref[...], HARD_SHARE, 0.0
    )
    for i in range(teachers):
        log_prob = (logits_ref[i] - norms[i]).astype(jnp.bfloat16).astype(jnp.float32)
        prob = jnp.exp(log_prob).astype(jnp.bfloat16).astype(jnp.float32)
        target = target + ((1.0 - HARD_SHARE) * weights[i]) * prob
    prob = jnp.exp(student_ref[...] - lse[:, at : at + 1])
    residual_ref[...] = (prob - target).astype(jnp.bfloat16)


def grad_body(hidden_ref, residual_ref, out_ref):
    out_ref[...] = jnp.dot(hidden_ref[...], residual_ref[...], preferred_element_type=jnp.float32)


def fast(teacher_hidden, teacher_head, student_hidden, student_head, labels):
    teachers = lax.axis_size("teacher")
    shards = lax.axis_size("vocab")
    chips = teachers // 2
    rows, width = teacher_head.shape
    tokens = student_hidden.shape[0]
    piece = tokens // shards // 2
    block = tokens // teachers
    x = lax.axis_index("teacher") // 2
    core = lax.axis_index("teacher") % 2
    f32 = jnp.float32

    mine = teacher_hidden[0].reshape(2, piece, chips, 2, rows)
    parts = []
    for to in range(teachers):
        half = mine[to % 2, :, to // 2]
        parts.append(jnp.concatenate([half[:, to % 2], half[:, 1 - to % 2]], axis=1))
    spread = jnp.broadcast_to(jnp.stack(parts)[:, None], (teachers, shards, piece, 2 * rows))
    spread = spread.reshape(teachers * shards, piece, 2 * rows)
    came = lax.all_to_all(spread, ("teacher", "vocab"), 0, 0, tiled=True)
    came = came.reshape(teachers, chips, block, 2 * rows)

    student_hidden, student_head, teacher_head, labels, _ = lax.optimization_barrier(
        (student_hidden, student_head, teacher_head, labels, spread)
    )
    sib_head = swap(teacher_head, "teacher", 1)
    sib_labels = swap(labels, "teacher", 1)
    ordered = student_hidden.reshape(chips, shards // chips, 2, piece, rows).transpose(0, 2, 1, 3, 4)
    ordered = ordered.reshape(tokens, rows)
    student = jnp.dot(ordered, student_head, preferred_element_type=f32).reshape(chips, 2, block, width)
    student_own = lax.dynamic_index_in_dim(student, core, 1, keepdims=False)
    student_sib = lax.dynamic_index_in_dim(student, 1 - core, 1, keepdims=False)
    student = student_own + swap(student_sib, "teacher", 1)
    student_own = lax.dynamic_index_in_dim(student, x, 0, keepdims=False)
    student_far = lax.dynamic_index_in_dim(student, 1 - x, 0, keepdims=False)
    student = student_own + swap(student_far, "teacher", 2)
    ordered_t = ordered.T

    step = min(width, 512)

    def partial(which):
        return call(
            functools.partial(partial_body, step),
            jax.ShapeDtypeStruct((teachers, block, width), f32),
            (which.reshape(1).astype(jnp.int32), came, teacher_head, sib_head),
            in_specs=[SMEM, VMEM, VMEM, VMEM],
            out_specs=VMEM,
            flops=2 * teachers * block * 2 * rows * width,
            moved=4 * rows * width,
        )

    sent = partial(1 - x).astype(jnp.float16)
    other = swap(sent, "teacher", 2).astype(f32)
    kept = partial(x)

    logits, stats = call(
        stats_body,
        (
            jax.ShapeDtypeStruct((teachers, block, width), f32),
            jax.ShapeDtypeStruct((2, block, LANES), f32),
        ),
        (kept, other, student),
        in_specs=[VMEM] * 3,
        out_specs=(VMEM, VMEM),
    )
    mask = 1
    while mask < shards:
        stats = merge(stats, swap(stats, "vocab", mask))
        mask *= 2

    pair = jnp.where(core == 0, jnp.stack([labels, sib_labels]), jnp.stack([sib_labels, labels]))
    chosen = lax.dynamic_index_in_dim(
        pair.reshape(shards // chips, 2, piece), core, 1, keepdims=False
    ).reshape(block, 1)
    local_label = chosen - lax.axis_index("vocab") * width
    entries = teachers * teachers + teachers
    small, residual = call(
        residual_body,
        (
            jax.ShapeDtypeStruct((-(-entries // 8) * 8, LANES), f32),
            jax.ShapeDtypeStruct((block, width), jnp.bfloat16),
        ),
        (logits, student, stats, local_label),
        in_specs=[VMEM] * 4,
        out_specs=(VMEM, VMEM),
    )
    gathered = lax.all_gather(residual, "teacher", axis=0, tiled=True)
    grad = call(
        grad_body,
        jax.ShapeDtypeStruct((rows, width), f32),
        (ordered_t, gathered),
        grid=(width // step,),
        in_specs=[
            pl.BlockSpec((rows, tokens), lambda i: (0, 0)),
            pl.BlockSpec((tokens, step), lambda i: (0, i)),
        ],
        out_specs=pl.BlockSpec((rows, step), lambda i: (0, i)),
        flops=2 * rows * tokens * width,
        moved=4 * rows * width,
    )

    small = small[:, :block]
    sib_small = swap(small, "teacher", 1)
    first = jnp.where(core == 0, small, sib_small).reshape(-1, 2, shards // chips // 2, piece)
    second = jnp.where(core == 0, sib_small, small).reshape(-1, 2, shards // chips // 2, piece)
    first = jnp.where(core == 0, first[:, 0], first[:, 1])
    second = jnp.where(core == 0, second[:, 0], second[:, 1])
    small = jnp.stack([first, second], axis=2).reshape(-1, block)
    cross = small[: teachers * teachers].T.reshape(block, teachers, teachers)
    return cross, small[teachers * teachers : entries].T, grad


def normalizer(logits):
    highest = lax.pmax(jnp.max(logits, axis=1), "vocab")
    summed = lax.psum(jnp.sum(jnp.exp(logits - highest[:, None]), axis=1), "vocab")
    return highest + jnp.log(summed)


def general(teacher_hidden, teacher_head, student_hidden, student_head, labels):
    teachers = lax.axis_size("teacher")
    block_rows = student_hidden.shape[0] // teachers
    shard_width = teacher_head.shape[1]
    gathered = lax.all_gather(teacher_hidden, "vocab", axis=1, tiled=True)
    logits = jnp.dot(
        gathered[0],
        lax.all_gather(teacher_head, "teacher", axis=0, tiled=True),
        preferred_element_type=jnp.float32,
    )
    log_prob = (logits - normalizer(logits)[:, None]).astype(jnp.bfloat16)
    exchanged = lax.all_to_all(log_prob[None], "teacher", split_axis=1, concat_axis=0, tiled=True)
    teacher_prob = jnp.exp(exchanged.astype(jnp.float32)).astype(jnp.bfloat16)
    cross_local = -jnp.einsum("itv,jtv->tij", teacher_prob, exchanged, preferred_element_type=jnp.float32)
    cross_matrix = lax.psum(cross_local, "vocab")
    inverse = 1.0 / (1.0 + jnp.mean(cross_matrix, axis=1))
    weights = inverse / jnp.sum(inverse, axis=1, keepdims=True)
    soft_mix = jnp.sum(weights.T[:, :, None] * teacher_prob.astype(jnp.float32), axis=0)
    col_offset = lax.axis_index("vocab") * shard_width
    columns = lax.broadcasted_iota(jnp.int32, (block_rows, shard_width), 1) + col_offset
    onehot = (columns == labels[:, None]).astype(jnp.float32)
    target = (1.0 - HARD_SHARE) * soft_mix + HARD_SHARE * onehot
    student_logits = lax.psum_scatter(
        jnp.dot(student_hidden, student_head, preferred_element_type=jnp.float32),
        "teacher",
        scatter_dimension=0,
        tiled=True,
    )
    student_prob = jnp.exp(student_logits - normalizer(student_logits)[:, None])
    residual = (student_prob - target).astype(jnp.bfloat16)
    student_grad = lax.dot_general(
        student_hidden,
        lax.all_gather(residual, "teacher", axis=0, tiled=True),
        (((0,), (0,)), ((), ())),
        preferred_element_type=jnp.float32,
    )
    return (cross_matrix, weights * teachers, student_grad)


def solution(mesh):
    body = fast if mesh.shape["teacher"] == 4 and mesh.shape["vocab"] == 8 else general
    return jax.shard_map(
        body,
        mesh=mesh,
        in_specs=(
            P("teacher", "vocab", None),
            P("teacher", "vocab"),
            P(None, "teacher"),
            P("teacher", "vocab"),
            P("teacher"),
        ),
        out_specs=(P("teacher", None, None), P("teacher", None), P("teacher", "vocab")),
        check_vma=False,
    )
```

```python
import functools

import jax
import jax.numpy as jnp
from jax import lax
from jax.experimental import pallas as pl
from jax.experimental.pallas import tpu as pltpu
from jax.sharding import PartitionSpec as P

HARD_SHARE = 0.3
LANES = 128


def swap(value, axis, mask):
    count = lax.axis_size(axis)
    return lax.ppermute(value, axis, [(i, i ^ mask) for i in range(count)])


def call(body, outs, args, grid=None, in_specs=None, out_specs=None, scratch=(), flops=0, moved=0, limit=16):
    extra = {} if grid is None else {"grid": grid}
    if in_specs is not None:
        extra["in_specs"] = in_specs
    if out_specs is not None:
        extra["out_specs"] = out_specs
    return pl.pallas_call(
        body,
        out_shape=outs,
        scratch_shapes=list(scratch),
        compiler_params=pltpu.CompilerParams(vmem_limit_bytes=limit * 1024 * 1024),
        cost_estimate=pl.CostEstimate(flops=flops, bytes_accessed=moved, transcendentals=0),
        **extra,
    )(*args)


VMEM = pl.BlockSpec(memory_space=pltpu.VMEM)


def split_body(hidden_ref, keep_ref, give_ref):
    piece = keep_ref.shape[0]
    core = lax.axis_index("teacher") % 2
    value = hidden_ref[...].astype(jnp.float32)
    low, high = value[:piece], value[piece:]
    keep_ref[...] = jnp.where(core == 0, low, high).astype(keep_ref.dtype)
    give_ref[...] = jnp.where(core == 0, high, low).astype(give_ref.dtype)


def halve_body(own_ref, sib_ref, keep_ref, give_ref):
    depth = keep_ref.shape[2]
    half = depth // 2
    x = lax.axis_index("teacher") // 2
    core = lax.axis_index("teacher") % 2
    own = own_ref[...].astype(jnp.float32)
    sib = sib_ref[...].astype(jnp.float32)
    for at, value in enumerate((jnp.where(core == 0, own, sib), jnp.where(core == 0, sib, own))):
        low, high = value[:, :depth], value[:, depth:]
        for ref, part in ((keep_ref, jnp.where(x == 0, low, high)), (give_ref, jnp.where(x == 0, high, low))):
            lead, trail = part[:, :half], part[:, half:]
            ref[at, :, :half] = jnp.where(core == 0, lead, trail).astype(ref.dtype)
            ref[at, :, half:] = jnp.where(core == 0, trail, lead).astype(ref.dtype)


def order_body(own_ref, far_ref, out_ref):
    x = lax.axis_index("teacher") // 2
    count = own_ref.shape[0]
    for i in range(count):
        out_ref[x * count + i] = own_ref[i]
        out_ref[(1 - x) * count + i] = far_ref[i]


def assemble_body(*refs):
    pieces, (away_ref, stay_ref, buf) = refs[:-3], refs[-3:]
    teachers, near = away_ref.shape[:2]
    x = lax.axis_index("teacher") // 2
    level = lax.axis_index("vocab") // 2
    for mask, piece_ref in enumerate(pieces):
        buf[level ^ mask] = piece_ref[...]
    for i in range(teachers):
        for j in range(near):
            away_ref[i, j] = buf[(1 - x) * near + j, i]
            stay_ref[i, j] = buf[x * near + j, i]


def partial_body(*refs):
    count = (len(refs) - 2) // 2
    hidden_refs, (own_ref, sib_ref), out_refs = refs[:count], refs[count : count + 2], refs[count + 2 :]
    half, width = own_ref.shape
    step = min(width, 512)
    rows = [ref[...] for ref in hidden_refs]
    rows = rows[0] if count == 1 else jnp.concatenate(rows, axis=0)
    for at in range(0, width, step):
        value = jnp.dot(rows[:, :half], own_ref[:, at : at + step], preferred_element_type=jnp.float32)
        value += jnp.dot(rows[:, half:], sib_ref[:, at : at + step], preferred_element_type=jnp.float32)
        value = value.reshape(count, *out_refs[0].shape[:2], step)
        for which, out_ref in enumerate(out_refs):
            out_ref[:, :, at : at + step] = value[which]


def student_body(hidden_ref, head_ref, keep_ref, give_ref, turned_ref):
    core = lax.axis_index("teacher") % 2
    chips, block, _ = keep_ref.shape
    value = jnp.dot(hidden_ref[...], head_ref[...], preferred_element_type=jnp.float32)
    near = 2
    piece = block // near // 2
    tall = hidden_ref[...].astype(jnp.float32)

    def place(x, level, side, c):
        return (((x * near + level) * 2 + side) * 2 + c) * piece

    for x in range(chips):
        for side in range(2):
            for level in range(near):
                low = value[place(x, level, side, 0) :][:piece]
                high = value[place(x, level, side, 1) :][:piece]
                to = (side * near + level) * piece
                keep_ref[x, to : to + piece] = jnp.where(core == 0, low, high)
                give_ref[x, to : to + piece] = jnp.where(core == 0, high, low)

    @pl.when(pl.program_id(0) == 0)
    def _():
        ordered = [
            tall[place(x, level, side, c) :][:piece]
            for x in range(chips)
            for c in range(2)
            for side in range(2)
            for level in range(near)
        ]
        turned_ref[...] = jnp.concatenate(ordered, axis=0).T.astype(turned_ref.dtype)


def sum_body(own_ref, sib_ref, keep_ref, give_ref):
    x = lax.axis_index("teacher") // 2
    keep_ref[...] = own_ref[x] + sib_ref[x]
    give_ref[...] = own_ref[1 - x] + sib_ref[1 - x]


def stats_body(part, logits_ref, student_ref, stats_ref):
    side = lax.axis_index("vocab") % 2
    teachers, rows, _ = logits_ref.shape
    lane = lax.broadcasted_iota(jnp.int32, (rows, LANES), 1)
    lse = jnp.zeros((rows, LANES), jnp.float32)
    mean = jnp.zeros((rows, LANES), jnp.float32)
    tops = [jnp.max(logits_ref[i], axis=1, keepdims=True) for i in range(teachers)]
    for i in range(teachers):
        weight = jnp.exp(logits_ref[i] - tops[i])
        total = jnp.sum(weight, axis=1, keepdims=True)
        group = (lane >= i * teachers) & (lane < (i + 1) * teachers)
        lse = jnp.where(group, tops[i] + jnp.log(total), lse)
        for j in range(teachers):
            local = jnp.sum(weight * (logits_ref[j] - tops[j]), axis=1, keepdims=True) / total + tops[j]
            mean = jnp.where(lane == i * teachers + j, local, mean)
    place = side if part == 0 else 1 - side
    value = student_ref[pl.ds(pl.multiple_of(place * rows, rows), rows)]
    top = jnp.max(value, axis=1, keepdims=True)
    total = jnp.sum(jnp.exp(value - top), axis=1, keepdims=True)
    stats_ref[0] = jnp.where(lane == teachers * teachers, top + jnp.log(total), lse)
    stats_ref[1] = mean


def merge(one, two):
    high = jnp.maximum(one[0], two[0])
    low = jnp.minimum(one[0], two[0])
    both = high + jnp.log1p(jnp.exp(low - high))
    return jnp.stack([both, jnp.exp(one[0] - both) * one[1] + jnp.exp(two[0] - both) * two[1]])


def residual_body(
    own_ref, other_ref, student_ref, stats_ref, label_ref, sib_label_ref, small_ref, residual_ref, weight_ref
):
    side = lax.axis_index("vocab") % 2
    core = lax.axis_index("teacher") % 2
    teachers, group, width = own_ref.shape
    rows = 2 * group
    lane = lax.broadcasted_iota(jnp.int32, (rows, LANES), 1)
    lse, mean = stats_ref[0], stats_ref[1]
    small = jnp.zeros((rows, LANES), jnp.float32)
    inverse = []
    for j in range(teachers):
        norm = lse[:, j * teachers : j * teachers + 1]
        spread = jnp.zeros((rows, 1), jnp.float32)
        for i in range(teachers):
            at = i * teachers + j
            entry = norm - mean[:, at : at + 1]
            small = jnp.where(lane == at, entry, small)
            spread = spread + entry
        inverse.append(1.0 / (1.0 + spread * (1.0 / teachers)))
    total = inverse[0]
    for i in range(1, teachers):
        total = total + inverse[i]
    at = teachers * teachers
    for i in range(teachers):
        small = jnp.where(lane == at + i, inverse[i] / total * teachers, small)
    weight_ref[...] = small
    square = jnp.concatenate([small, jnp.zeros((LANES - rows, LANES), jnp.float32)], axis=0)
    small_ref[...] = square.T[: small_ref.shape[0]]
    piece = rows // 4
    token = lax.broadcasted_iota(jnp.int32, (rows, rows), 0)
    source = lax.broadcasted_iota(jnp.int32, (rows, rows), 1)
    hit = source == token // (2 * piece) * (2 * piece) + core * piece + token % piece
    mine = token // piece % 2 == core
    label = jnp.where(hit, jnp.where(mine, label_ref[...], sib_label_ref[...]), 0)
    label = jnp.sum(label, axis=1, keepdims=True) - lax.axis_index("vocab") * width
    label_at = lambda place: jnp.where(place == 0, label[:group], label[group:])
    for part, logits_ref in enumerate((own_ref, other_ref)):
        place = side if part == 0 else 1 - side
        span = pl.ds(pl.multiple_of(place * group, group), group)
        norms = stats_ref[0, span]
        weights = weight_ref[span]
        target = jnp.where(
            lax.broadcasted_iota(jnp.int32, (group, width), 1) == label_at(place), HARD_SHARE, 0.0
        )
        for i in range(teachers):
            norm = norms[:, i * teachers : i * teachers + 1]
            log_prob = (logits_ref[i] - norm).astype(jnp.bfloat16).astype(jnp.float32)
            prob = jnp.exp(log_prob).astype(jnp.bfloat16).astype(jnp.float32)
            target = target + ((1.0 - HARD_SHARE) / teachers * weights[:, at + i : at + i + 1]) * prob
        prob = jnp.exp(student_ref[span] - norms[:, at : at + 1])
        residual_ref[span] = (prob - target).astype(jnp.bfloat16)


def grad_body(hidden_ref, residual_ref, small_ref, sib_ref, grad_ref, cross_ref, agree_ref):
    core = lax.axis_index("teacher") % 2
    grad_ref[...] = jnp.dot(hidden_ref[...], residual_ref[...], preferred_element_type=jnp.float32)

    @pl.when(pl.program_id(0) == 0)
    def _():
        block = cross_ref.shape[1]
        piece = block // 4
        source = lax.broadcasted_iota(jnp.int32, (LANES, block), 0)
        token = lax.broadcasted_iota(jnp.int32, (LANES, block), 1)
        hit = source == token // (2 * piece) * (2 * piece) + core * piece + token % piece
        mine = token // piece % 2 == core
        placed = sum(
            jnp.dot(
                ref[...],
                jnp.where(hit & which, 1.0, 0.0),
                preferred_element_type=jnp.float32,
                precision=lax.Precision.HIGHEST,
            )
            for ref, which in ((small_ref, mine), (sib_ref, jnp.logical_not(mine)))
        )
        count = cross_ref.shape[0]
        cross_ref[...] = placed[:count]
        agree_ref[...] = placed[count : count + agree_ref.shape[0]]


def fast(teacher_hidden, teacher_head, student_hidden, student_head, labels):
    teachers = lax.axis_size("teacher")
    shards = lax.axis_size("vocab")
    chips = teachers // 2
    rows, width = teacher_head.shape
    tokens = student_hidden.shape[0]
    near = shards // 2 // chips
    piece = tokens // shards // 2
    block = tokens // teachers
    group = block // 2
    f32 = jnp.float32
    kind = teacher_hidden.dtype
    shape = jax.ShapeDtypeStruct

    def local(body, outs, args, **extra):
        return call(body, outs, args, in_specs=[VMEM] * len(args), out_specs=(VMEM,) * len(outs), **extra)

    keep, give = local(split_body, (shape((piece, teachers * rows), kind),) * 2, (teacher_hidden[0],))
    sib = swap(give, "teacher", 1)
    teacher_head, labels, keep = lax.optimization_barrier((teacher_head, labels, keep))
    sib_head = swap(teacher_head, "teacher", 1)
    sib_labels = swap(labels, "teacher", 1)
    keep, give = local(halve_body, (shape((2, piece, 2 * rows), kind),) * 2, (keep, sib))
    student_hidden, student_head, keep = lax.optimization_barrier((student_hidden, student_head, keep))
    (part,) = local(
        order_body, (shape((teachers, piece, 2 * rows), kind),), (keep, swap(give, "teacher", 2))
    )
    parts = [part] + [swap(part, "vocab", 2 * mask) for mask in range(1, shards // 2)]
    away, stay = local(
        assemble_body,
        (shape((teachers, near, piece, 2 * rows), kind),) * 2,
        parts,
        scratch=[pltpu.VMEM((shards // 2, teachers, piece, 2 * rows), kind)],
    )
    away = away.reshape(teachers * group, 2 * rows)
    stay = stay.reshape(teachers * group, 2 * rows)

    step = min(width, 512)
    whole = lambda i: (0, 0)
    keep, give, turned = call(
        student_body,
        (shape((chips, block, width), f32),) * 2 + (shape((rows, tokens), student_hidden.dtype),),
        (student_hidden, student_head),
        grid=(width // step,),
        in_specs=[pl.BlockSpec((tokens, rows), whole), pl.BlockSpec((rows, step), lambda i: (0, i))],
        out_specs=(pl.BlockSpec((chips, block, step), lambda i: (0, 0, i)),) * 2
        + (pl.BlockSpec((rows, tokens), whole),),
        flops=2 * tokens * rows * width,
        moved=2 * rows * width,
    )
    keep, give = local(sum_body, (shape((block, width), f32),) * 2, (keep, swap(give, "teacher", 1)))
    student = keep + swap(give, "teacher", 2)

    flat = shape((teachers, group, width), f32)

    def partial(*hidden):
        return local(
            partial_body,
            (flat,) * len(hidden),
            (*hidden, teacher_head, sib_head),
            flops=2 * len(hidden) * teachers * group * 2 * rows * width,
            moved=4 * rows * width,
        )

    other_away = swap(away, "vocab", 1)
    other_stay = swap(stay, "vocab", 1)
    sent, kept = partial(away, stay)
    far = swap(sent.astype(jnp.float16), "teacher", 2)
    (other_sent,) = partial(other_away)
    other_far = swap(other_sent.astype(jnp.float16), "teacher", 2)
    (other_kept,) = partial(other_stay)

    logits = [kept + far.astype(f32), other_kept + other_far.astype(f32)]
    stats = [
        local(functools.partial(stats_body, at), (shape((2, group, LANES), f32),), (logits[at], student))[0]
        for at in range(2)
    ]
    side = lax.axis_index("vocab") % 2
    stats = jnp.where(side == 0, jnp.concatenate(stats, axis=1), jnp.concatenate(stats[::-1], axis=1))
    mask = 1
    while mask < shards:
        stats = merge(stats, swap(stats, "vocab", mask))
        mask *= 2

    entries = teachers * teachers + teachers
    small, residual = local(
        residual_body,
        (shape((-(-entries // 8) * 8, LANES), f32), shape((block, width), jnp.bfloat16)),
        (*logits, student, stats, labels.reshape(1, block), sib_labels.reshape(1, block)),
        scratch=[pltpu.VMEM((block, LANES), f32)],
    )
    sib_small = swap(small, "teacher", 1)
    gathered = lax.all_gather(residual, "teacher", axis=0, tiled=True)
    grad, cross, agree = call(
        grad_body,
        (
            shape((rows, width), f32),
            shape((teachers * teachers, block), f32),
            shape((teachers, block), f32),
        ),
        (turned, gathered, small, sib_small),
        grid=(width // step,),
        in_specs=[
            pl.BlockSpec((rows, tokens), whole),
            pl.BlockSpec((tokens, step), lambda i: (0, i)),
            pl.BlockSpec(small.shape, whole),
            pl.BlockSpec(small.shape, whole),
        ],
        out_specs=(
            pl.BlockSpec((rows, step), lambda i: (0, i)),
            pl.BlockSpec((teachers * teachers, block), whole),
            pl.BlockSpec((teachers, block), whole),
        ),
        flops=2 * rows * tokens * width,
        moved=4 * rows * width,
    )
    return cross.T.reshape(block, teachers, teachers), agree.T, grad


def normalizer(logits):
    highest = lax.pmax(jnp.max(logits, axis=1), "vocab")
    summed = lax.psum(jnp.sum(jnp.exp(logits - highest[:, None]), axis=1), "vocab")
    return highest + jnp.log(summed)


def general(teacher_hidden, teacher_head, student_hidden, student_head, labels):
    teachers = lax.axis_size("teacher")
    block_rows = student_hidden.shape[0] // teachers
    shard_width = teacher_head.shape[1]
    gathered = lax.all_gather(teacher_hidden, "vocab", axis=1, tiled=True)
    logits = jnp.dot(
        gathered[0],
        lax.all_gather(teacher_head, "teacher", axis=0, tiled=True),
        preferred_element_type=jnp.float32,
    )
    log_prob = (logits - normalizer(logits)[:, None]).astype(jnp.bfloat16)
    exchanged = lax.all_to_all(log_prob[None], "teacher", split_axis=1, concat_axis=0, tiled=True)
    teacher_prob = jnp.exp(exchanged.astype(jnp.float32)).astype(jnp.bfloat16)
    cross_local = -jnp.einsum("itv,jtv->tij", teacher_prob, exchanged, preferred_element_type=jnp.float32)
    cross_matrix = lax.psum(cross_local, "vocab")
    inverse = 1.0 / (1.0 + jnp.mean(cross_matrix, axis=1))
    weights = inverse / jnp.sum(inverse, axis=1, keepdims=True)
    soft_mix = jnp.sum(weights.T[:, :, None] * teacher_prob.astype(jnp.float32), axis=0)
    col_offset = lax.axis_index("vocab") * shard_width
    columns = lax.broadcasted_iota(jnp.int32, (block_rows, shard_width), 1) + col_offset
    onehot = (columns == labels[:, None]).astype(jnp.float32)
    target = (1.0 - HARD_SHARE) * soft_mix + HARD_SHARE * onehot
    student_logits = lax.psum_scatter(
        jnp.dot(student_hidden, student_head, preferred_element_type=jnp.float32),
        "teacher",
        scatter_dimension=0,
        tiled=True,
    )
    student_prob = jnp.exp(student_logits - normalizer(student_logits)[:, None])
    residual = (student_prob - target).astype(jnp.bfloat16)
    student_grad = lax.dot_general(
        student_hidden,
        lax.all_gather(residual, "teacher", axis=0, tiled=True),
        (((0,), (0,)), ((), ())),
        preferred_element_type=jnp.float32,
    )
    return (cross_matrix, weights * teachers, student_grad)


def solution(mesh):
    body = fast if mesh.shape["teacher"] == 4 and mesh.shape["vocab"] == 8 else general
    return jax.shard_map(
        body,
        mesh=mesh,
        in_specs=(
            P("teacher", "vocab", None),
            P("teacher", "vocab"),
            P(None, "teacher"),
            P("teacher", "vocab"),
            P("teacher"),
        ),
        out_specs=(P("teacher", None, None), P("teacher", None), P("teacher", "vocab")),
        check_vma=False,
    )
```

```python
import functools

import jax
import jax.numpy as jnp
from jax import lax
from jax.experimental import pallas as pl
from jax.experimental.pallas import tpu as pltpu
from jax.sharding import PartitionSpec as P

HARD_SHARE = 0.3
LANES = 128
TOP = 32767.0


def swap(value, axis, mask):
    count = lax.axis_size(axis)
    return lax.ppermute(value, axis, [(i, i ^ mask) for i in range(count)])


def call(body, outs, args, limit=16, scratch=(), **extra):
    return pl.pallas_call(
        body,
        out_shape=outs,
        scratch_shapes=list(scratch),
        compiler_params=pltpu.CompilerParams(vmem_limit_bytes=limit * 1024 * 1024),
        cost_estimate=pl.CostEstimate(flops=1, bytes_accessed=1, transcendentals=0),
        **extra,
    )(*args)


VMEM = pl.BlockSpec(memory_space=pltpu.VMEM)


def split_body(own_ref, far_ref, keep_ref, give_ref):
    piece, depth = keep_ref.shape[1:]
    half = depth // 2
    x = lax.axis_index("teacher") // 2
    core = lax.axis_index("teacher") % 2
    own = own_ref[...].astype(jnp.float32)
    far = far_ref[...].astype(jnp.float32)
    for at, value in enumerate((jnp.where(x == 0, own, far), jnp.where(x == 0, far, own))):
        value = jnp.where(x == 0, value[:, :depth], value[:, depth:])
        low, high = value[:piece], value[piece:]
        for ref, part, mine in (
            (keep_ref, jnp.where(core == 0, low, high), core),
            (give_ref, jnp.where(core == 0, high, low), 1 - core),
        ):
            lead, trail = part[:, :half], part[:, half:]
            ref[at, :, :half] = jnp.where(mine == 0, lead, trail).astype(ref.dtype)
            ref[at, :, half:] = jnp.where(mine == 0, trail, lead).astype(ref.dtype)


def order_body(own_ref, sib_ref, out_ref):
    core = lax.axis_index("teacher") % 2
    for i in range(own_ref.shape[0]):
        out_ref[2 * i + core] = own_ref[i]
        out_ref[2 * i + 1 - core] = sib_ref[i]


def assemble_body(*refs):
    pieces, (away_ref, stay_ref, buf) = refs[:-3], refs[-3:]
    teachers, near = away_ref.shape[:2]
    x = lax.axis_index("teacher") // 2
    level = lax.axis_index("vocab") // 2
    for mask, piece_ref in enumerate(pieces):
        buf[level ^ mask] = piece_ref[...]
    for i in range(teachers):
        for j in range(near):
            away_ref[i, j] = buf[(1 - x) * near + j, i]
            stay_ref[i, j] = buf[x * near + j, i]


def encode(value, code_ref, at):
    width = value.shape[1]
    count = jnp.floor(jnp.max(jnp.abs(value), axis=1, keepdims=True) * 0.5) + 1.0
    code = jnp.floor(value * (TOP * 0.5 / count) + 0.5)
    code_ref[(*at, slice(None), slice(0, width))] = code.astype(jnp.int32).astype(code_ref.dtype)
    count = jnp.broadcast_to(count, (value.shape[0], LANES))
    code_ref[(*at, slice(None), slice(width, width + LANES))] = count.astype(jnp.int32).astype(code_ref.dtype)


def decode(code):
    code = code.astype(jnp.int32).astype(jnp.float32)
    width = code.shape[1] - LANES
    return code[:, :width] * (code[:, width : width + 1] * (2.0 / TOP))


def partial_body(code, *refs):
    count = (len(refs) - 2 - code) // 2
    hidden_refs, (own_ref, sib_ref), out_refs = refs[:count], refs[count : count + 2], refs[count + 2 :]
    if code:
        code_ref, out_refs = out_refs[0], (out_refs[-1], *out_refs[1:-1])
    half, width = own_ref.shape
    step = min(width, 512)
    rows = [ref[...] for ref in hidden_refs]
    rows = rows[0] if count == 1 else jnp.concatenate(rows, axis=0)
    for at in range(0, width, step):
        value = jnp.dot(rows[:, :half], own_ref[:, at : at + step], preferred_element_type=jnp.float32)
        value += jnp.dot(rows[:, half:], sib_ref[:, at : at + step], preferred_element_type=jnp.float32)
        value = value.reshape(count, *out_refs[0].shape[:2], step)
        for which, out_ref in enumerate(out_refs):
            out_ref[:, :, at : at + step] = value[which]
    if code:
        for i in range(code_ref.shape[0]):
            encode(out_refs[0][i], code_ref, (i,))


def student_body(hidden_ref, head_ref, keep_ref, *refs):
    give_refs, turned_ref = refs[:-1], refs[-1]
    core = lax.axis_index("teacher") % 2
    chips, block, width = keep_ref.shape
    step = give_refs[0].shape[2]
    near = 2
    piece = block // near // 2
    tall = hidden_ref[...].astype(jnp.float32)

    def place(x, level, side, c):
        return (((x * near + level) * 2 + side) * 2 + c) * piece

    ordered = [
        tall[place(x, level, side, c) :][:piece]
        for x in range(chips)
        for c in range(2)
        for side in range(2)
        for level in range(near)
    ]
    turned_ref[...] = jnp.concatenate(ordered, axis=0).T.astype(turned_ref.dtype)
    for at, give_ref in enumerate(give_refs):
        columns = slice(at * step, (at + 1) * step)
        value = jnp.dot(hidden_ref[...], head_ref[:, columns], preferred_element_type=jnp.float32)
        for x in range(chips):
            for side in range(2):
                for level in range(near):
                    low = value[place(x, level, side, 0) :][:piece]
                    high = value[place(x, level, side, 1) :][:piece]
                    to = (side * near + level) * piece
                    keep_ref[x, to : to + piece, columns] = jnp.where(core == 0, low, high)
                    give_ref[x, to : to + piece] = jnp.where(core == 0, high, low)


def sum_body(cuts, own_ref, *refs):
    sib_refs, (keep_ref, give_ref) = refs[:cuts], refs[cuts:]
    x = lax.axis_index("teacher") // 2
    keep_ref[...] = own_ref[x] + jnp.concatenate([ref[x] for ref in sib_refs], axis=1)
    encode(own_ref[1 - x] + jnp.concatenate([ref[1 - x] for ref in sib_refs], axis=1), give_ref, ())


def stats_body(part, kept_ref, came_ref, student_ref, far_ref, *refs):
    logits_ref, student_out_ref, stats_ref = refs[-3:]
    side = lax.axis_index("vocab") % 2
    teachers, rows, _ = logits_ref.shape
    for i in range(teachers):
        logits_ref[i] = kept_ref[i] + decode(came_ref[i])
    lane = lax.broadcasted_iota(jnp.int32, (rows, LANES), 1)
    lse = jnp.zeros((rows, LANES), jnp.float32)
    mean = jnp.zeros((rows, LANES), jnp.float32)
    tops = [jnp.max(logits_ref[i], axis=1, keepdims=True) for i in range(teachers)]
    for i in range(teachers):
        weight = jnp.exp(logits_ref[i] - tops[i])
        total = jnp.sum(weight, axis=1, keepdims=True)
        group = (lane >= i * teachers) & (lane < (i + 1) * teachers)
        lse = jnp.where(group, tops[i] + jnp.log(total), lse)
        for j in range(teachers):
            local = jnp.sum(weight * (logits_ref[j] - tops[j]), axis=1, keepdims=True) / total + tops[j]
            mean = jnp.where(lane == i * teachers + j, local, mean)
    place = side if part == 0 else 1 - side
    span = pl.ds(pl.multiple_of(place * rows, rows), rows)
    value = student_ref[span] + decode(far_ref[span])
    student_out_ref[...] = value
    top = jnp.max(value, axis=1, keepdims=True)
    total = jnp.sum(jnp.exp(value - top), axis=1, keepdims=True)
    lse = jnp.where(lane == teachers * teachers, top + jnp.log(total), lse)
    if part == 0:
        stats_ref[0] = lse
        stats_ref[1] = mean
    else:
        first_ref = refs[0]
        own = pl.ds(pl.multiple_of(side * rows, rows), rows)
        for at, value in enumerate((lse, mean)):
            stats_ref[at, own] = first_ref[at]
            stats_ref[at, span] = value


def merge(one, two):
    high = jnp.maximum(one[0], two[0])
    low = jnp.minimum(one[0], two[0])
    both = high + jnp.log1p(jnp.exp(low - high))
    return jnp.stack([both, jnp.exp(one[0] - both) * one[1] + jnp.exp(two[0] - both) * two[1]])


def residual_body(
    own_ref, other_ref, student_ref, other_student_ref, stats_ref, label_ref, sib_label_ref, small_ref, residual_ref, weight_ref
):
    side = lax.axis_index("vocab") % 2
    core = lax.axis_index("teacher") % 2
    teachers, group, width = own_ref.shape
    rows = 2 * group
    lane = lax.broadcasted_iota(jnp.int32, (rows, LANES), 1)
    lse, mean = stats_ref[0], stats_ref[1]
    small = jnp.zeros((rows, LANES), jnp.float32)
    inverse = []
    for j in range(teachers):
        norm = lse[:, j * teachers : j * teachers + 1]
        spread = jnp.zeros((rows, 1), jnp.float32)
        for i in range(teachers):
            at = i * teachers + j
            entry = norm - mean[:, at : at + 1]
            small = jnp.where(lane == at, entry, small)
            spread = spread + entry
        inverse.append(1.0 / (1.0 + spread * (1.0 / teachers)))
    total = inverse[0]
    for i in range(1, teachers):
        total = total + inverse[i]
    at = teachers * teachers
    for i in range(teachers):
        small = jnp.where(lane == at + i, inverse[i] / total * teachers, small)
    weight_ref[...] = small
    square = jnp.concatenate([small, jnp.zeros((LANES - rows, LANES), jnp.float32)], axis=0)
    small_ref[...] = square.T[: small_ref.shape[0]]
    piece = rows // 4
    token = lax.broadcasted_iota(jnp.int32, (rows, rows), 0)
    source = lax.broadcasted_iota(jnp.int32, (rows, rows), 1)
    hit = source == token // (2 * piece) * (2 * piece) + core * piece + token % piece
    mine = token // piece % 2 == core
    label = jnp.where(hit, jnp.where(mine, label_ref[...], sib_label_ref[...]), 0)
    label = jnp.sum(label, axis=1, keepdims=True) - lax.axis_index("vocab") * width
    label_at = lambda place: jnp.where(place == 0, label[:group], label[group:])
    for part, (logits_ref, value_ref) in enumerate(((own_ref, student_ref), (other_ref, other_student_ref))):
        place = side if part == 0 else 1 - side
        span = pl.ds(pl.multiple_of(place * group, group), group)
        norms = stats_ref[0, span]
        weights = weight_ref[span]
        target = jnp.where(
            lax.broadcasted_iota(jnp.int32, (group, width), 1) == label_at(place), HARD_SHARE, 0.0
        )
        for i in range(teachers):
            norm = norms[:, i * teachers : i * teachers + 1]
            log_prob = (logits_ref[i] - norm).astype(jnp.bfloat16).astype(jnp.float32)
            prob = jnp.exp(log_prob).astype(jnp.bfloat16).astype(jnp.float32)
            target = target + ((1.0 - HARD_SHARE) / teachers * weights[:, at + i : at + i + 1]) * prob
        prob = jnp.exp(value_ref[...] - norms[:, at : at + 1])
        residual_ref[span] = (prob - target).astype(jnp.bfloat16)


def grad_body(hidden_ref, residual_ref, small_ref, sib_ref, grad_ref, cross_ref, agree_ref, buf, sems):
    parts, step, _ = buf.shape
    copies = []
    for at in range(parts):
        rows = pl.ds(at * step, step)
        buf[at] = jnp.dot(hidden_ref[rows], residual_ref[...], preferred_element_type=jnp.float32)
        copies.append(pltpu.make_async_copy(buf.at[at], grad_ref.at[rows], sems.at[at]))
        copies[at].start()
    core = lax.axis_index("teacher") % 2
    block = cross_ref.shape[1]
    piece = block // 4
    source = lax.broadcasted_iota(jnp.int32, (LANES, block), 0)
    token = lax.broadcasted_iota(jnp.int32, (LANES, block), 1)
    hit = source == token // (2 * piece) * (2 * piece) + core * piece + token % piece
    mine = token // piece % 2 == core
    placed = sum(
        jnp.dot(
            ref[...],
            jnp.where(hit & which, 1.0, 0.0),
            preferred_element_type=jnp.float32,
            precision=lax.Precision.HIGHEST,
        )
        for ref, which in ((small_ref, mine), (sib_ref, jnp.logical_not(mine)))
    )
    count = cross_ref.shape[0]
    cross_ref[...] = placed[:count]
    agree_ref[...] = placed[count : count + agree_ref.shape[0]]
    for copy in copies:
        copy.wait()


def fast(teacher_hidden, teacher_head, student_hidden, student_head, labels):
    teachers = lax.axis_size("teacher")
    shards = lax.axis_size("vocab")
    chips = teachers // 2
    rows, width = teacher_head.shape
    tokens = student_hidden.shape[0]
    near = shards // 2 // chips
    piece = tokens // shards // 2
    block = tokens // teachers
    group = block // 2
    f32 = jnp.float32
    kind = teacher_hidden.dtype
    shape = jax.ShapeDtypeStruct

    any_place = pl.BlockSpec(memory_space=pl.ANY)

    def local(body, outs, args, after=(), specs=None, **extra):
        specs = [VMEM] * len(args) if specs is None else specs
        skip = len(after)
        return call(
            (lambda *refs: body(*refs[skip:])) if after else body,
            outs,
            (*after, *args),
            in_specs=[any_place] * skip + specs,
            out_specs=(VMEM,) * len(outs),
            **extra,
        )

    own = teacher_hidden[0]
    far = swap(own, "teacher", 2)
    keep, give = local(split_body, (shape((2, piece, 2 * rows), kind),) * 2, (own, far))
    split = keep
    (part,) = local(order_body, (shape((teachers, piece, 2 * rows), kind),), (keep, swap(give, "teacher", 1)))
    parts = [part] + [swap(part, "vocab", 2 * mask) for mask in range(1, shards // 2)]
    sib_head = swap(teacher_head, "teacher", 1)
    sib_labels = swap(labels, "teacher", 1)
    cuts = max(1, min(4, width // LANES))
    mine, *others, turned = local(
        student_body,
        (
            shape((chips, block, width), f32),
            *(shape((chips, block, width // cuts), f32),) * cuts,
            shape((rows, tokens), student_hidden.dtype),
        ),
        (student_hidden, student_head),
        after=(),
    )
    others = [swap(value, "teacher", 1) for value in others]
    coded = functools.partial(shape, dtype=jnp.int16)
    student, give = local(
        functools.partial(sum_body, cuts),
        (shape((block, width), f32), coded((block, width + LANES))),
        (mine, *others),
        after=(sib_head,),
    )
    student_far = swap(give, "teacher", 2)
    away, stay = local(
        assemble_body,
        (shape((teachers, near, piece, 2 * rows), kind),) * 2,
        parts,
        scratch=[pltpu.VMEM((shards // 2, teachers, piece, 2 * rows), kind)],
    )
    away = away.reshape(teachers * group, 2 * rows)
    stay = stay.reshape(teachers * group, 2 * rows)

    flat = shape((teachers, group, width), f32)

    def partial(outs, *hidden):
        code = outs[0].dtype == jnp.int16
        return local(
            functools.partial(partial_body, int(code)),
            outs,
            (*hidden, teacher_head, sib_head),
            scratch=[pltpu.VMEM(flat.shape, f32)] if code else (),
        )

    code = coded((teachers, group, width + LANES))
    sent, kept = partial((code, flat), away, stay)
    sent, away, stay = lax.optimization_barrier((sent, away, stay))
    far = swap(sent, "teacher", 2)
    other_away = swap(away, "vocab", 1)
    other_away, stay, student_far = lax.optimization_barrier((other_away, stay, student_far))
    other_stay = swap(stay, "vocab", 1)
    (other_sent,) = partial((code,), other_away)
    other_far = swap(other_sent, "teacher", 2)
    (other_kept,) = partial((flat,), other_stay)

    outs = (flat, shape((group, width), f32))
    logits, mine, first = local(
        functools.partial(stats_body, 0), (*outs, shape((2, group, LANES), f32)), (kept, far, student, student_far)
    )
    other_logits, others, stats = local(
        functools.partial(stats_body, 1),
        (*outs, shape((2, block, LANES), f32)),
        (other_kept, other_far, student, student_far, first),
    )
    mask = 1
    while mask < shards:
        stats = merge(stats, swap(stats, "vocab", mask))
        mask *= 2

    entries = teachers * teachers + teachers
    small, residual = local(
        residual_body,
        (shape((-(-entries // 8) * 8, LANES), f32), shape((block, width), jnp.bfloat16)),
        (logits, other_logits, mine, others, stats, labels.reshape(1, block), sib_labels.reshape(1, block)),
        scratch=[pltpu.VMEM((block, LANES), f32)],
    )
    sib_small = swap(small, "teacher", 1)
    gathered = lax.all_gather(residual, "teacher", axis=0, tiled=True)
    parts = 8 if rows % 8 == 0 else 1
    grad, cross, agree = call(
        grad_body,
        (shape((rows, width), f32), shape((teachers * teachers, block), f32), shape((teachers, block), f32)),
        (turned, gathered, small, sib_small),
        in_specs=[VMEM] * 4,
        out_specs=(pl.BlockSpec(memory_space=pl.ANY), VMEM, VMEM),
        scratch=[pltpu.VMEM((parts, rows // parts, width), f32), pltpu.SemaphoreType.DMA((parts,))],
    )
    return cross.T.reshape(block, teachers, teachers), agree.T, grad


def normalizer(logits):
    highest = lax.pmax(jnp.max(logits, axis=1), "vocab")
    summed = lax.psum(jnp.sum(jnp.exp(logits - highest[:, None]), axis=1), "vocab")
    return highest + jnp.log(summed)


def general(teacher_hidden, teacher_head, student_hidden, student_head, labels):
    teachers = lax.axis_size("teacher")
    block_rows = student_hidden.shape[0] // teachers
    shard_width = teacher_head.shape[1]
    gathered = lax.all_gather(teacher_hidden, "vocab", axis=1, tiled=True)
    logits = jnp.dot(
        gathered[0],
        lax.all_gather(teacher_head, "teacher", axis=0, tiled=True),
        preferred_element_type=jnp.float32,
    )
    log_prob = (logits - normalizer(logits)[:, None]).astype(jnp.bfloat16)
    exchanged = lax.all_to_all(log_prob[None], "teacher", split_axis=1, concat_axis=0, tiled=True)
    teacher_prob = jnp.exp(exchanged.astype(jnp.float32)).astype(jnp.bfloat16)
    cross_local = -jnp.einsum("itv,jtv->tij", teacher_prob, exchanged, preferred_element_type=jnp.float32)
    cross_matrix = lax.psum(cross_local, "vocab")
    inverse = 1.0 / (1.0 + jnp.mean(cross_matrix, axis=1))
    weights = inverse / jnp.sum(inverse, axis=1, keepdims=True)
    soft_mix = jnp.sum(weights.T[:, :, None] * teacher_prob.astype(jnp.float32), axis=0)
    col_offset = lax.axis_index("vocab") * shard_width
    columns = lax.broadcasted_iota(jnp.int32, (block_rows, shard_width), 1) + col_offset
    onehot = (columns == labels[:, None]).astype(jnp.float32)
    target = (1.0 - HARD_SHARE) * soft_mix + HARD_SHARE * onehot
    student_logits = lax.psum_scatter(
        jnp.dot(student_hidden, student_head, preferred_element_type=jnp.float32),
        "teacher",
        scatter_dimension=0,
        tiled=True,
    )
    student_prob = jnp.exp(student_logits - normalizer(student_logits)[:, None])
    residual = (student_prob - target).astype(jnp.bfloat16)
    student_grad = lax.dot_general(
        student_hidden,
        lax.all_gather(residual, "teacher", axis=0, tiled=True),
        (((0,), (0,)), ((), ())),
        preferred_element_type=jnp.float32,
    )
    return (cross_matrix, weights * teachers, student_grad)


def solution(mesh):
    body = fast if mesh.shape["teacher"] == 4 and mesh.shape["vocab"] == 8 else general
    return jax.shard_map(
        body,
        mesh=mesh,
        in_specs=(
            P("teacher", "vocab", None),
            P("teacher", "vocab"),
            P(None, "teacher"),
            P("teacher", "vocab"),
            P("teacher"),
        ),
        out_specs=(P("teacher", None, None), P("teacher", None), P("teacher", "vocab")),
        check_vma=False,
    )
```

```python
import functools

import jax
import jax.numpy as jnp
from jax import lax
from jax.experimental import pallas as pl
from jax.experimental.pallas import tpu as pltpu
from jax.sharding import PartitionSpec as P

HARD_SHARE = 0.3
LANES = 128
TOP = 32767.0


def swap(value, axis, mask):
    count = lax.axis_size(axis)
    return lax.ppermute(value, axis, [(i, i ^ mask) for i in range(count)])


def call(body, outs, args, limit=16, scratch=(), **extra):
    return pl.pallas_call(
        body,
        out_shape=outs,
        scratch_shapes=list(scratch),
        compiler_params=pltpu.CompilerParams(vmem_limit_bytes=limit * 1024 * 1024),
        cost_estimate=pl.CostEstimate(flops=1, bytes_accessed=1, transcendentals=0),
        **extra,
    )(*args)


VMEM = pl.BlockSpec(memory_space=pltpu.VMEM)


def split_body(own_ref, far_ref, keep_ref, give_ref):
    piece, depth = keep_ref.shape[1:]
    half = depth // 2
    x = lax.axis_index("teacher") // 2
    core = lax.axis_index("teacher") % 2
    own = own_ref[...].astype(jnp.float32)
    far = far_ref[...].astype(jnp.float32)
    for at, value in enumerate((jnp.where(x == 0, own, far), jnp.where(x == 0, far, own))):
        value = jnp.where(x == 0, value[:, :depth], value[:, depth:])
        low, high = value[:piece], value[piece:]
        for ref, part, mine in (
            (keep_ref, jnp.where(core == 0, low, high), core),
            (give_ref, jnp.where(core == 0, high, low), 1 - core),
        ):
            lead, trail = part[:, :half], part[:, half:]
            ref[at, :, :half] = jnp.where(mine == 0, lead, trail).astype(ref.dtype)
            ref[at, :, half:] = jnp.where(mine == 0, trail, lead).astype(ref.dtype)


def order_body(own_ref, sib_ref, out_ref):
    core = lax.axis_index("teacher") % 2
    for i in range(own_ref.shape[0]):
        out_ref[2 * i + core] = own_ref[i]
        out_ref[2 * i + 1 - core] = sib_ref[i]


def assemble_body(*refs):
    pieces, (away_ref, stay_ref, buf) = refs[:-3], refs[-3:]
    teachers, near = away_ref.shape[:2]
    x = lax.axis_index("teacher") // 2
    level = lax.axis_index("vocab") // 2
    for mask, piece_ref in enumerate(pieces):
        buf[level ^ mask] = piece_ref[...]
    for i in range(teachers):
        for j in range(near):
            away_ref[i, j] = buf[(1 - x) * near + j, i]
            stay_ref[i, j] = buf[x * near + j, i]


def encode(value, code_ref, at):
    width = value.shape[1]
    count = jnp.floor(jnp.max(jnp.abs(value), axis=1, keepdims=True) * 0.5) + 1.0
    code = jnp.floor(value * (TOP * 0.5 / count) + 0.5)
    code_ref[(*at, slice(None), slice(0, width))] = code.astype(jnp.int32).astype(code_ref.dtype)
    count = jnp.broadcast_to(count, (value.shape[0], LANES))
    code_ref[(*at, slice(None), slice(width, width + LANES))] = count.astype(jnp.int32).astype(code_ref.dtype)


def decode(code):
    code = code.astype(jnp.int32).astype(jnp.float32)
    width = code.shape[1] - LANES
    return code[:, :width] * (code[:, width : width + 1] * (2.0 / TOP))


def partial_body(code, *refs):
    count = (len(refs) - 2 - code) // 2
    hidden_refs, (own_ref, sib_ref), out_refs = refs[:count], refs[count : count + 2], refs[count + 2 :]
    if code:
        code_ref, out_refs = out_refs[0], (out_refs[-1], *out_refs[1:-1])
    half, width = own_ref.shape
    step = min(width, 512)
    rows = [ref[...] for ref in hidden_refs]
    rows = rows[0] if count == 1 else jnp.concatenate(rows, axis=0)
    for at in range(0, width, step):
        value = jnp.dot(rows[:, :half], own_ref[:, at : at + step], preferred_element_type=jnp.float32)
        value += jnp.dot(rows[:, half:], sib_ref[:, at : at + step], preferred_element_type=jnp.float32)
        value = value.reshape(count, *out_refs[0].shape[:2], step)
        for which, out_ref in enumerate(out_refs):
            out_ref[:, :, at : at + step] = value[which]
    if code:
        for i in range(code_ref.shape[0]):
            encode(out_refs[0][i], code_ref, (i,))


def student_body(hidden_ref, head_ref, keep_ref, *refs):
    give_refs, turned_ref = refs[:-1], refs[-1]
    core = lax.axis_index("teacher") % 2
    chips, block, width = keep_ref.shape
    step = give_refs[0].shape[2]
    near = 2
    piece = block // near // 2
    tall = hidden_ref[...].astype(jnp.float32)

    def place(x, level, side, c):
        return (((x * near + level) * 2 + side) * 2 + c) * piece

    ordered = [
        tall[place(x, level, side, c) :][:piece]
        for x in range(chips)
        for c in range(2)
        for side in range(2)
        for level in range(near)
    ]
    turned_ref[...] = jnp.concatenate(ordered, axis=0).T.astype(turned_ref.dtype)
    for at, give_ref in enumerate(give_refs):
        columns = slice(at * step, (at + 1) * step)
        value = jnp.dot(hidden_ref[...], head_ref[:, columns], preferred_element_type=jnp.float32)
        for x in range(chips):
            for side in range(2):
                for level in range(near):
                    low = value[place(x, level, side, 0) :][:piece]
                    high = value[place(x, level, side, 1) :][:piece]
                    to = (side * near + level) * piece
                    keep_ref[x, to : to + piece, columns] = jnp.where(core == 0, low, high)
                    give_ref[x, to : to + piece] = jnp.where(core == 0, high, low)


def sum_body(cuts, own_ref, *refs):
    sib_refs, (keep_ref, give_ref) = refs[:cuts], refs[cuts:]
    x = lax.axis_index("teacher") // 2
    keep_ref[...] = own_ref[x] + jnp.concatenate([ref[x] for ref in sib_refs], axis=1)
    encode(own_ref[1 - x] + jnp.concatenate([ref[1 - x] for ref in sib_refs], axis=1), give_ref, ())


def stats_body(part, kept_ref, came_ref, student_ref, far_ref, *refs):
    logits_ref, student_out_ref, stats_ref = refs[-3:]
    side = lax.axis_index("vocab") % 2
    teachers, rows, _ = logits_ref.shape
    for i in range(teachers):
        logits_ref[i] = kept_ref[i] + decode(came_ref[i])
    lane = lax.broadcasted_iota(jnp.int32, (rows, LANES), 1)
    lse = jnp.zeros((rows, LANES), jnp.float32)
    mean = jnp.zeros((rows, LANES), jnp.float32)
    tops = [jnp.max(logits_ref[i], axis=1, keepdims=True) for i in range(teachers)]
    for i in range(teachers):
        weight = jnp.exp(logits_ref[i] - tops[i])
        total = jnp.sum(weight, axis=1, keepdims=True)
        group = (lane >= i * teachers) & (lane < (i + 1) * teachers)
        lse = jnp.where(group, tops[i] + jnp.log(total), lse)
        for j in range(teachers):
            local = jnp.sum(weight * (logits_ref[j] - tops[j]), axis=1, keepdims=True) / total + tops[j]
            mean = jnp.where(lane == LANES // 2 + i * teachers + j, local, mean)
    place = side if part == 0 else 1 - side
    span = pl.ds(pl.multiple_of(place * rows, rows), rows)
    value = student_ref[span] + decode(far_ref[span])
    student_out_ref[...] = value
    top = jnp.max(value, axis=1, keepdims=True)
    total = jnp.sum(jnp.exp(value - top), axis=1, keepdims=True)
    lse = jnp.where(lane == teachers * teachers, top + jnp.log(total), lse)
    value = jnp.where(lane < LANES // 2, lse, mean)
    if part == 0:
        stats_ref[...] = value
    else:
        stats_ref[pl.ds(pl.multiple_of(side * rows, rows), rows)] = refs[0][...]
        stats_ref[span] = value


def merge_body(one_ref, two_ref, out_ref):
    half = LANES // 2
    first = lax.broadcasted_iota(jnp.int32, one_ref.shape, 1) < half
    one, two = one_ref[...], two_ref[...]
    one_lse = jnp.where(first, one, pltpu.roll(one, half, 1))
    two_lse = jnp.where(first, two, pltpu.roll(two, half, 1))
    high = jnp.maximum(one_lse, two_lse)
    both = high + jnp.log(1.0 + jnp.exp(jnp.minimum(one_lse, two_lse) - high))
    mean = jnp.exp(one_lse - both) * one + jnp.exp(two_lse - both) * two
    out_ref[...] = jnp.where(first, both, mean)


def residual_body(
    own_ref, other_ref, student_ref, other_student_ref, stats_ref, label_ref, sib_label_ref, small_ref, residual_ref, weight_ref
):
    side = lax.axis_index("vocab") % 2
    core = lax.axis_index("teacher") % 2
    teachers, group, width = own_ref.shape
    rows = 2 * group
    lane = lax.broadcasted_iota(jnp.int32, (rows, LANES), 1)
    lse, mean = stats_ref[:, : LANES // 2], stats_ref[:, LANES // 2 :]
    small = jnp.zeros((rows, LANES), jnp.float32)
    inverse = []
    for j in range(teachers):
        norm = lse[:, j * teachers : j * teachers + 1]
        spread = jnp.zeros((rows, 1), jnp.float32)
        for i in range(teachers):
            at = i * teachers + j
            entry = norm - mean[:, at : at + 1]
            small = jnp.where(lane == at, entry, small)
            spread = spread + entry
        inverse.append(1.0 / (1.0 + spread * (1.0 / teachers)))
    total = inverse[0]
    for i in range(1, teachers):
        total = total + inverse[i]
    at = teachers * teachers
    for i in range(teachers):
        small = jnp.where(lane == at + i, inverse[i] / total * teachers, small)
    weight_ref[...] = small
    square = jnp.concatenate([small, jnp.zeros((LANES - rows, LANES), jnp.float32)], axis=0)
    small_ref[...] = square.T[: small_ref.shape[0]]
    piece = rows // 4
    token = lax.broadcasted_iota(jnp.int32, (rows, rows), 0)
    source = lax.broadcasted_iota(jnp.int32, (rows, rows), 1)
    hit = source == token // (2 * piece) * (2 * piece) + core * piece + token % piece
    mine = token // piece % 2 == core
    label = jnp.where(hit, jnp.where(mine, label_ref[...], sib_label_ref[...]), 0)
    label = jnp.sum(label, axis=1, keepdims=True) - lax.axis_index("vocab") * width
    label_at = lambda place: jnp.where(place == 0, label[:group], label[group:])
    for part, (logits_ref, value_ref) in enumerate(((own_ref, student_ref), (other_ref, other_student_ref))):
        place = side if part == 0 else 1 - side
        span = pl.ds(pl.multiple_of(place * group, group), group)
        norms = stats_ref[span]
        weights = weight_ref[span]
        target = jnp.where(
            lax.broadcasted_iota(jnp.int32, (group, width), 1) == label_at(place), HARD_SHARE, 0.0
        )
        for i in range(teachers):
            norm = norms[:, i * teachers : i * teachers + 1]
            log_prob = (logits_ref[i] - norm).astype(jnp.bfloat16).astype(jnp.float32)
            prob = jnp.exp(log_prob).astype(jnp.bfloat16).astype(jnp.float32)
            target = target + ((1.0 - HARD_SHARE) / teachers * weights[:, at + i : at + i + 1]) * prob
        prob = jnp.exp(value_ref[...] - norms[:, at : at + 1])
        residual_ref[span] = (prob - target).astype(jnp.bfloat16)


def grad_body(hidden_ref, *refs):
    count = lax.axis_size("teacher")
    residual_refs, (small_ref, sib_ref, grad_ref, cross_ref, agree_ref) = refs[:-10], refs[-10:-5]
    buf, rows_ref, cross_buf, agree_buf, sems = refs[-5:]
    if len(residual_refs) > 1:
        me = lax.axis_index("teacher")
        size = rows_ref.shape[0] // count
        for mask, ref in enumerate(residual_refs):
            rows_ref[pl.ds(pl.multiple_of((me ^ mask) * size, size), size)] = ref[...]
    else:
        rows_ref = residual_refs[0]
    parts, step, _ = buf.shape
    copies = []

    def send(value, ref):
        copies.append(pltpu.make_async_copy(value, ref, sems.at[len(copies)]))
        copies[-1].start()

    for at in range(parts):
        rows = pl.ds(at * step, step)
        buf[at] = jnp.dot(hidden_ref[rows], rows_ref[...], preferred_element_type=jnp.float32)
        send(buf.at[at], grad_ref.at[rows])
        if at == 0:
            core = lax.axis_index("teacher") % 2
            block = cross_buf.shape[1]
            piece = block // 4
            source = lax.broadcasted_iota(jnp.int32, (LANES, block), 0)
            token = lax.broadcasted_iota(jnp.int32, (LANES, block), 1)
            hit = source == token // (2 * piece) * (2 * piece) + core * piece + token % piece
            mine = token // piece % 2 == core
            placed = sum(
                jnp.dot(
                    ref[...],
                    jnp.where(hit & which, 1.0, 0.0),
                    preferred_element_type=jnp.float32,
                    precision=lax.Precision.HIGHEST,
                )
                for ref, which in ((small_ref, mine), (sib_ref, jnp.logical_not(mine)))
            )
            entries = cross_buf.shape[0]
            cross_buf[...] = placed[:entries]
            agree_buf[...] = placed[entries : entries + agree_buf.shape[0]]
            send(cross_buf, cross_ref)
            send(agree_buf, agree_ref)
    for copy in copies:
        copy.wait()


def fast(teacher_hidden, teacher_head, student_hidden, student_head, labels):
    teachers = lax.axis_size("teacher")
    shards = lax.axis_size("vocab")
    chips = teachers // 2
    rows, width = teacher_head.shape
    tokens = student_hidden.shape[0]
    near = shards // 2 // chips
    piece = tokens // shards // 2
    block = tokens // teachers
    group = block // 2
    f32 = jnp.float32
    kind = teacher_hidden.dtype
    shape = jax.ShapeDtypeStruct

    any_place = pl.BlockSpec(memory_space=pl.ANY)

    def local(body, outs, args, after=(), specs=None, **extra):
        specs = [VMEM] * len(args) if specs is None else specs
        skip = len(after)
        return call(
            (lambda *refs: body(*refs[skip:])) if after else body,
            outs,
            (*after, *args),
            in_specs=[any_place] * skip + specs,
            out_specs=(VMEM,) * len(outs),
            **extra,
        )

    own = teacher_hidden[0]
    far = swap(own, "teacher", 2)
    keep, give = local(split_body, (shape((2, piece, 2 * rows), kind),) * 2, (own, far))
    split = keep
    (part,) = local(order_body, (shape((teachers, piece, 2 * rows), kind),), (keep, swap(give, "teacher", 1)))
    parts = [part] + [swap(part, "vocab", 2 * mask) for mask in range(1, shards // 2)]
    sib_head = swap(teacher_head, "teacher", 1)
    sib_labels = swap(labels, "teacher", 1)
    cuts = max(1, min(4, width // LANES))
    mine, *others, turned = local(
        student_body,
        (
            shape((chips, block, width), f32),
            *(shape((chips, block, width // cuts), f32),) * cuts,
            shape((rows, tokens), student_hidden.dtype),
        ),
        (student_hidden, student_head),
        after=(),
    )
    others = [swap(value, "teacher", 1) for value in others]
    coded = functools.partial(shape, dtype=jnp.int16)
    student, give = local(
        functools.partial(sum_body, cuts),
        (shape((block, width), f32), coded((block, width + LANES))),
        (mine, *others),
        after=(sib_head,),
    )
    student_far = swap(give, "teacher", 2)
    away, stay = local(
        assemble_body,
        (shape((teachers, near, piece, 2 * rows), kind),) * 2,
        parts,
        scratch=[pltpu.VMEM((shards // 2, teachers, piece, 2 * rows), kind)],
    )
    away = away.reshape(teachers * group, 2 * rows)
    stay = stay.reshape(teachers * group, 2 * rows)

    flat = shape((teachers, group, width), f32)

    def partial(outs, *hidden):
        code = outs[0].dtype == jnp.int16
        return local(
            functools.partial(partial_body, int(code)),
            outs,
            (*hidden, teacher_head, sib_head),
            scratch=[pltpu.VMEM(flat.shape, f32)] if code else (),
        )

    code = coded((teachers, group, width + LANES))
    sent, kept = partial((code, flat), away, stay)
    sent, away, stay = lax.optimization_barrier((sent, away, stay))
    far = swap(sent, "teacher", 2)
    other_away = swap(away, "vocab", 1)
    other_away, stay, student_far = lax.optimization_barrier((other_away, stay, student_far))
    other_stay = swap(stay, "vocab", 1)
    (other_sent,) = partial((code,), other_away)
    other_far = swap(other_sent, "teacher", 2)
    (other_kept,) = partial((flat,), other_stay)

    outs = (flat, shape((group, width), f32))
    logits, mine, first = local(
        functools.partial(stats_body, 0), (*outs, shape((group, LANES), f32)), (kept, far, student, student_far)
    )
    other_logits, others, stats = local(
        functools.partial(stats_body, 1),
        (*outs, shape((block, LANES), f32)),
        (other_kept, other_far, student, student_far, first),
    )
    mask = 1
    while mask < shards:
        (stats,) = local(merge_body, (shape((block, LANES), f32),), (stats, swap(stats, "vocab", mask)))
        mask *= 2

    entries = teachers * teachers + teachers
    small, residual = local(
        residual_body,
        (shape((-(-entries // 8) * 8, LANES), f32), shape((block, width), jnp.bfloat16)),
        (logits, other_logits, mine, others, stats, labels.reshape(1, block), sib_labels.reshape(1, block)),
        scratch=[pltpu.VMEM((block, LANES), f32)],
    )
    sib_small = swap(small, "teacher", 1)
    sib_residual = swap(residual, "teacher", 1)
    far_residual = swap(residual, "teacher", 2)
    residuals = (residual, sib_residual, far_residual, swap(far_residual, "teacher", 1))
    parts = 8 if rows % 8 == 0 else 1
    squares = shape((teachers * teachers, block), f32), shape((teachers, block), f32)
    grad, cross, agree = call(
        grad_body,
        (shape((rows, width), f32), *squares),
        (turned, *residuals, small, sib_small),
        in_specs=[VMEM] * (3 + len(residuals)),
        out_specs=(any_place,) * 3,
        scratch=[
            pltpu.VMEM((parts, rows // parts, width), f32),
            pltpu.VMEM((tokens, width), residual.dtype),
            *(pltpu.VMEM(square.shape, f32) for square in squares),
            pltpu.SemaphoreType.DMA((parts + 2,)),
        ],
    )
    return cross.T.reshape(block, teachers, teachers), agree.T, grad


def normalizer(logits):
    highest = lax.pmax(jnp.max(logits, axis=1), "vocab")
    summed = lax.psum(jnp.sum(jnp.exp(logits - highest[:, None]), axis=1), "vocab")
    return highest + jnp.log(summed)


def general(teacher_hidden, teacher_head, student_hidden, student_head, labels):
    teachers = lax.axis_size("teacher")
    block_rows = student_hidden.shape[0] // teachers
    shard_width = teacher_head.shape[1]
    gathered = lax.all_gather(teacher_hidden, "vocab", axis=1, tiled=True)
    logits = jnp.dot(
        gathered[0],
        lax.all_gather(teacher_head, "teacher", axis=0, tiled=True),
        preferred_element_type=jnp.float32,
    )
    log_prob = (logits - normalizer(logits)[:, None]).astype(jnp.bfloat16)
    exchanged = lax.all_to_all(log_prob[None], "teacher", split_axis=1, concat_axis=0, tiled=True)
    teacher_prob = jnp.exp(exchanged.astype(jnp.float32)).astype(jnp.bfloat16)
    cross_local = -jnp.einsum("itv,jtv->tij", teacher_prob, exchanged, preferred_element_type=jnp.float32)
    cross_matrix = lax.psum(cross_local, "vocab")
    inverse = 1.0 / (1.0 + jnp.mean(cross_matrix, axis=1))
    weights = inverse / jnp.sum(inverse, axis=1, keepdims=True)
    soft_mix = jnp.sum(weights.T[:, :, None] * teacher_prob.astype(jnp.float32), axis=0)
    col_offset = lax.axis_index("vocab") * shard_width
    columns = lax.broadcasted_iota(jnp.int32, (block_rows, shard_width), 1) + col_offset
    onehot = (columns == labels[:, None]).astype(jnp.float32)
    target = (1.0 - HARD_SHARE) * soft_mix + HARD_SHARE * onehot
    student_logits = lax.psum_scatter(
        jnp.dot(student_hidden, student_head, preferred_element_type=jnp.float32),
        "teacher",
        scatter_dimension=0,
        tiled=True,
    )
    student_prob = jnp.exp(student_logits - normalizer(student_logits)[:, None])
    residual = (student_prob - target).astype(jnp.bfloat16)
    student_grad = lax.dot_general(
        student_hidden,
        lax.all_gather(residual, "teacher", axis=0, tiled=True),
        (((0,), (0,)), ((), ())),
        preferred_element_type=jnp.float32,
    )
    return (cross_matrix, weights * teachers, student_grad)


def solution(mesh):
    body = fast if mesh.shape["teacher"] == 4 and mesh.shape["vocab"] == 8 else general
    return jax.shard_map(
        body,
        mesh=mesh,
        in_specs=(
            P("teacher", "vocab", None),
            P("teacher", "vocab"),
            P(None, "teacher"),
            P("teacher", "vocab"),
            P("teacher"),
        ),
        out_specs=(P("teacher", None, None), P("teacher", None), P("teacher", "vocab")),
        check_vma=False,
    )
```

```python
import functools

import jax
import jax.numpy as jnp
from jax import lax
from jax.experimental import pallas as pl
from jax.experimental.pallas import tpu as pltpu
from jax.sharding import PartitionSpec as P

HARD_SHARE = 0.3
LANES = 128
TOP = 32767.0


def swap(value, axis, mask):
    count = lax.axis_size(axis)
    return lax.ppermute(value, axis, [(i, i ^ mask) for i in range(count)])


def call(body, outs, args, limit=16, scratch=(), **extra):
    return pl.pallas_call(
        body,
        out_shape=outs,
        scratch_shapes=list(scratch),
        compiler_params=pltpu.CompilerParams(vmem_limit_bytes=limit * 1024 * 1024),
        cost_estimate=pl.CostEstimate(flops=1, bytes_accessed=1, transcendentals=0),
        **extra,
    )(*args)


VMEM = pl.BlockSpec(memory_space=pltpu.VMEM)


def split_body(own_ref, far_ref, keep_ref, give_ref):
    piece, depth = keep_ref.shape[1:]
    half = depth // 2
    x = lax.axis_index("teacher") // 2
    core = lax.axis_index("teacher") % 2
    own = own_ref[...].astype(jnp.float32)
    far = far_ref[...].astype(jnp.float32)
    for at, value in enumerate((jnp.where(x == 0, own, far), jnp.where(x == 0, far, own))):
        value = jnp.where(x == 0, value[:, :depth], value[:, depth:])
        low, high = value[:piece], value[piece:]
        for ref, part, mine in (
            (keep_ref, jnp.where(core == 0, low, high), core),
            (give_ref, jnp.where(core == 0, high, low), 1 - core),
        ):
            lead, trail = part[:, :half], part[:, half:]
            ref[at, :, :half] = jnp.where(mine == 0, lead, trail).astype(ref.dtype)
            ref[at, :, half:] = jnp.where(mine == 0, trail, lead).astype(ref.dtype)


def order_body(own_ref, sib_ref, out_ref):
    core = lax.axis_index("teacher") % 2
    for i in range(own_ref.shape[0]):
        out_ref[2 * i + core] = own_ref[i]
        out_ref[2 * i + 1 - core] = sib_ref[i]


def assemble_body(*refs):
    pieces, (away_ref, stay_ref, buf) = refs[:-3], refs[-3:]
    teachers, near = away_ref.shape[:2]
    x = lax.axis_index("teacher") // 2
    level = lax.axis_index("vocab") // 2
    for mask, piece_ref in enumerate(pieces):
        buf[level ^ mask] = piece_ref[...]
    for i in range(teachers):
        for j in range(near):
            away_ref[i, j] = buf[(1 - x) * near + j, i]
            stay_ref[i, j] = buf[x * near + j, i]


def encode(value, code_ref, at):
    width = value.shape[1]
    count = jnp.floor(jnp.max(jnp.abs(value), axis=1, keepdims=True) * 0.5) + 1.0
    code = jnp.floor(value * (TOP * 0.5 / count) + 0.5)
    code_ref[(*at, slice(None), slice(0, width))] = code.astype(jnp.int32).astype(code_ref.dtype)
    count = jnp.broadcast_to(count, (value.shape[0], LANES))
    code_ref[(*at, slice(None), slice(width, width + LANES))] = count.astype(jnp.int32).astype(code_ref.dtype)


def decode(code):
    code = code.astype(jnp.int32).astype(jnp.float32)
    width = code.shape[1] - LANES
    return code[:, :width] * (code[:, width : width + 1] * (2.0 / TOP))


def partial_body(code, *refs):
    count = (len(refs) - 2 - code) // 2
    hidden_refs, (own_ref, sib_ref), out_refs = refs[:count], refs[count : count + 2], refs[count + 2 :]
    if code:
        code_ref, out_refs = out_refs[0], (out_refs[-1], *out_refs[1:-1])
    half, width = own_ref.shape
    step = min(width, 512)
    rows = [ref[...] for ref in hidden_refs]
    rows = rows[0] if count == 1 else jnp.concatenate(rows, axis=0)
    for at in range(0, width, step):
        value = jnp.dot(rows[:, :half], own_ref[:, at : at + step], preferred_element_type=jnp.float32)
        value += jnp.dot(rows[:, half:], sib_ref[:, at : at + step], preferred_element_type=jnp.float32)
        value = value.reshape(count, *out_refs[0].shape[:2], step)
        for which, out_ref in enumerate(out_refs):
            out_ref[:, :, at : at + step] = value[which]
    if code:
        for i in range(code_ref.shape[0]):
            encode(out_refs[0][i], code_ref, (i,))


def student_body(hidden_ref, head_ref, keep_ref, *refs):
    give_refs, turned_ref = refs[:-1], refs[-1]
    core = lax.axis_index("teacher") % 2
    chips, block, width = keep_ref.shape
    step = give_refs[0].shape[2]
    near = 2
    piece = block // near // 2
    tall = hidden_ref[...].astype(jnp.float32)

    def place(x, level, side, c):
        return (((x * near + level) * 2 + side) * 2 + c) * piece

    ordered = [
        tall[place(x, level, side, c) :][:piece]
        for x in range(chips)
        for c in range(2)
        for side in range(2)
        for level in range(near)
    ]
    turned_ref[...] = jnp.concatenate(ordered, axis=0).T.astype(turned_ref.dtype)
    for at, give_ref in enumerate(give_refs):
        columns = slice(at * step, (at + 1) * step)
        value = jnp.dot(hidden_ref[...], head_ref[:, columns], preferred_element_type=jnp.float32)
        for x in range(chips):
            for side in range(2):
                for level in range(near):
                    low = value[place(x, level, side, 0) :][:piece]
                    high = value[place(x, level, side, 1) :][:piece]
                    to = (side * near + level) * piece
                    keep_ref[x, to : to + piece, columns] = jnp.where(core == 0, low, high)
                    give_ref[x, to : to + piece] = jnp.where(core == 0, high, low)


def sum_body(cuts, own_ref, *refs):
    sib_refs, (keep_ref, give_ref) = refs[:cuts], refs[cuts:]
    x = lax.axis_index("teacher") // 2
    keep_ref[...] = own_ref[x] + jnp.concatenate([ref[x] for ref in sib_refs], axis=1)
    encode(own_ref[1 - x] + jnp.concatenate([ref[1 - x] for ref in sib_refs], axis=1), give_ref, ())


def stats_body(part, kept_ref, came_ref, student_ref, far_ref, *refs):
    logits_ref, student_out_ref, stats_ref = refs[-3:]
    side = lax.axis_index("vocab") % 2
    teachers, rows, _ = logits_ref.shape
    for i in range(teachers):
        logits_ref[i] = kept_ref[i] + decode(came_ref[i])
    lane = lax.broadcasted_iota(jnp.int32, (rows, LANES), 1)
    lse = jnp.zeros((rows, LANES), jnp.float32)
    mean = jnp.zeros((rows, LANES), jnp.float32)
    tops = [jnp.max(logits_ref[i], axis=1, keepdims=True) for i in range(teachers)]
    for i in range(teachers):
        weight = jnp.exp(logits_ref[i] - tops[i])
        total = jnp.sum(weight, axis=1, keepdims=True)
        group = (lane >= i * teachers) & (lane < (i + 1) * teachers)
        lse = jnp.where(group, tops[i] + jnp.log(total), lse)
        for j in range(teachers):
            local = jnp.sum(weight * (logits_ref[j] - tops[j]), axis=1, keepdims=True) / total + tops[j]
            mean = jnp.where(lane == LANES // 2 + i * teachers + j, local, mean)
    place = side if part == 0 else 1 - side
    span = pl.ds(pl.multiple_of(place * rows, rows), rows)
    value = student_ref[span] + decode(far_ref[span])
    student_out_ref[...] = value
    top = jnp.max(value, axis=1, keepdims=True)
    total = jnp.sum(jnp.exp(value - top), axis=1, keepdims=True)
    lse = jnp.where(lane == teachers * teachers, top + jnp.log(total), lse)
    value = jnp.where(lane < LANES // 2, lse, mean)
    if part == 0:
        stats_ref[...] = value
    else:
        stats_ref[pl.ds(pl.multiple_of(side * rows, rows), rows)] = refs[0][...]
        stats_ref[span] = value


def merge_body(one_ref, two_ref, out_ref):
    half = LANES // 2
    first = lax.broadcasted_iota(jnp.int32, one_ref.shape, 1) < half
    one, two = one_ref[...], two_ref[...]
    one_lse = jnp.where(first, one, pltpu.roll(one, half, 1))
    two_lse = jnp.where(first, two, pltpu.roll(two, half, 1))
    high = jnp.maximum(one_lse, two_lse)
    both = high + jnp.log(1.0 + jnp.exp(jnp.minimum(one_lse, two_lse) - high))
    mean = jnp.exp(one_lse - both) * one + jnp.exp(two_lse - both) * two
    out_ref[...] = jnp.where(first, both, mean)


def residual_body(
    own_ref, other_ref, student_ref, other_student_ref, stats_ref, label_ref, sib_label_ref, small_ref, residual_ref, weight_ref
):
    side = lax.axis_index("vocab") % 2
    core = lax.axis_index("teacher") % 2
    teachers, group, width = own_ref.shape
    rows = 2 * group
    lane = lax.broadcasted_iota(jnp.int32, (rows, LANES), 1)
    lse, mean = stats_ref[:, : LANES // 2], stats_ref[:, LANES // 2 :]
    small = jnp.zeros((rows, LANES), jnp.float32)
    inverse = []
    for j in range(teachers):
        norm = lse[:, j * teachers : j * teachers + 1]
        spread = jnp.zeros((rows, 1), jnp.float32)
        for i in range(teachers):
            at = i * teachers + j
            entry = norm - mean[:, at : at + 1]
            small = jnp.where(lane == at, entry, small)
            spread = spread + entry
        inverse.append(1.0 / (1.0 + spread * (1.0 / teachers)))
    total = inverse[0]
    for i in range(1, teachers):
        total = total + inverse[i]
    at = teachers * teachers
    for i in range(teachers):
        small = jnp.where(lane == at + i, inverse[i] / total * teachers, small)
    weight_ref[...] = small
    square = jnp.concatenate([small, jnp.zeros((LANES - rows, LANES), jnp.float32)], axis=0)
    small_ref[...] = square.T[: small_ref.shape[0]]
    piece = rows // 4
    token = lax.broadcasted_iota(jnp.int32, (rows, rows), 0)
    source = lax.broadcasted_iota(jnp.int32, (rows, rows), 1)
    hit = source == token // (2 * piece) * (2 * piece) + core * piece + token % piece
    mine = token // piece % 2 == core
    label = jnp.where(hit, jnp.where(mine, label_ref[...], sib_label_ref[...]), 0)
    label = jnp.sum(label, axis=1, keepdims=True) - lax.axis_index("vocab") * width
    label_at = lambda place: jnp.where(place == 0, label[:group], label[group:])
    for part, (logits_ref, value_ref) in enumerate(((own_ref, student_ref), (other_ref, other_student_ref))):
        place = side if part == 0 else 1 - side
        span = pl.ds(pl.multiple_of(place * group, group), group)
        norms = stats_ref[span]
        weights = weight_ref[span]
        target = jnp.where(
            lax.broadcasted_iota(jnp.int32, (group, width), 1) == label_at(place), HARD_SHARE, 0.0
        )
        for i in range(teachers):
            norm = norms[:, i * teachers : i * teachers + 1]
            log_prob = (logits_ref[i] - norm).astype(jnp.bfloat16).astype(jnp.float32)
            prob = jnp.exp(log_prob).astype(jnp.bfloat16).astype(jnp.float32)
            target = target + ((1.0 - HARD_SHARE) / teachers * weights[:, at + i : at + i + 1]) * prob
        prob = jnp.exp(value_ref[...] - norms[:, at : at + 1])
        residual_ref[span] = (prob - target).astype(jnp.bfloat16)


def grad_body(hidden_ref, *refs):
    count = lax.axis_size("teacher")
    residual_refs, (small_ref, sib_ref, grad_ref, cross_ref, agree_ref) = refs[:-10], refs[-10:-5]
    buf, rows_ref, cross_buf, agree_buf, sems = refs[-5:]
    if len(residual_refs) > 1:
        me = lax.axis_index("teacher")
        size = rows_ref.shape[0] // count
        for mask, ref in enumerate(residual_refs):
            rows_ref[pl.ds(pl.multiple_of((me ^ mask) * size, size), size)] = ref[...]
    else:
        rows_ref = residual_refs[0]
    parts, step, _ = buf.shape
    copies = []

    def send(value, ref):
        copies.append(pltpu.make_async_copy(value, ref, sems.at[len(copies)]))
        copies[-1].start()

    for at in range(parts):
        rows = pl.ds(at * step, step)
        buf[at] = jnp.dot(hidden_ref[rows], rows_ref[...], preferred_element_type=jnp.float32)
        send(buf.at[at], grad_ref.at[rows])
        if at == 0:
            core = lax.axis_index("teacher") % 2
            block = cross_buf.shape[1]
            piece = block // 4
            source = lax.broadcasted_iota(jnp.int32, (LANES, block), 0)
            token = lax.broadcasted_iota(jnp.int32, (LANES, block), 1)
            hit = source == token // (2 * piece) * (2 * piece) + core * piece + token % piece
            mine = token // piece % 2 == core
            placed = sum(
                jnp.dot(
                    ref[...],
                    jnp.where(hit & which, 1.0, 0.0),
                    preferred_element_type=jnp.float32,
                    precision=lax.Precision.HIGHEST,
                )
                for ref, which in ((small_ref, mine), (sib_ref, jnp.logical_not(mine)))
            )
            entries = cross_buf.shape[0]
            cross_buf[...] = placed[:entries]
            agree_buf[...] = placed[entries : entries + agree_buf.shape[0]]
            send(cross_buf, cross_ref)
            send(agree_buf, agree_ref)
    for copy in copies:
        copy.wait()


def fast(teacher_hidden, teacher_head, student_hidden, student_head, labels):
    teachers = lax.axis_size("teacher")
    shards = lax.axis_size("vocab")
    chips = teachers // 2
    rows, width = teacher_head.shape
    tokens = student_hidden.shape[0]
    near = shards // 2 // chips
    piece = tokens // shards // 2
    block = tokens // teachers
    group = block // 2
    f32 = jnp.float32
    kind = teacher_hidden.dtype
    shape = jax.ShapeDtypeStruct

    any_place = pl.BlockSpec(memory_space=pl.ANY)

    def local(body, outs, args, after=(), specs=None, **extra):
        specs = [VMEM] * len(args) if specs is None else specs
        skip = len(after)
        return call(
            (lambda *refs: body(*refs[skip:])) if after else body,
            outs,
            (*after, *args),
            in_specs=[any_place] * skip + specs,
            out_specs=(VMEM,) * len(outs),
            **extra,
        )

    own = teacher_hidden[0]
    far = swap(own, "teacher", 2)
    keep, give = local(split_body, (shape((2, piece, 2 * rows), kind),) * 2, (own, far))
    split = keep
    (part,) = local(order_body, (shape((teachers, piece, 2 * rows), kind),), (keep, swap(give, "teacher", 1)))
    parts = [part] + [swap(part, "vocab", 2 * mask) for mask in range(1, shards // 2)]
    sib_head = swap(teacher_head, "teacher", 1)
    sib_labels = swap(labels, "teacher", 1)
    cuts = max(1, min(4, width // LANES))
    mine, *others, turned = local(
        student_body,
        (
            shape((chips, block, width), f32),
            *(shape((chips, block, width // cuts), f32),) * cuts,
            shape((rows, tokens), student_hidden.dtype),
        ),
        (student_hidden, student_head),
        after=(),
    )
    others = [swap(value, "teacher", 1) for value in others]
    coded = functools.partial(shape, dtype=jnp.int16)
    student, give = local(
        functools.partial(sum_body, cuts),
        (shape((block, width), f32), coded((block, width + LANES))),
        (mine, *others),
        after=(sib_head,),
    )
    student_far = swap(give, "teacher", 2)
    away, stay = local(
        assemble_body,
        (shape((teachers, near, piece, 2 * rows), kind),) * 2,
        parts,
        scratch=[pltpu.VMEM((shards // 2, teachers, piece, 2 * rows), kind)],
    )
    away = away.reshape(teachers * group, 2 * rows)
    stay = stay.reshape(teachers * group, 2 * rows)

    flat = shape((teachers, group, width), f32)

    def partial(outs, *hidden):
        code = outs[0].dtype == jnp.int16
        return local(
            functools.partial(partial_body, int(code)),
            outs,
            (*hidden, teacher_head, sib_head),
            scratch=[pltpu.VMEM(flat.shape, f32)] if code else (),
        )

    code = coded((teachers, group, width + LANES))
    sent, kept = partial((code, flat), away, stay)
    sent, away, stay = lax.optimization_barrier((sent, away, stay))
    far = swap(sent, "teacher", 2)
    other_away = swap(away, "vocab", 1)
    stay, far = lax.optimization_barrier((stay, far))
    other_away, student_far = lax.optimization_barrier((other_away, student_far))
    other_stay = swap(stay, "vocab", 1)
    (other_sent,) = partial((code,), other_away)
    other_far = swap(other_sent, "teacher", 2)
    (other_kept,) = partial((flat,), other_stay)

    outs = (flat, shape((group, width), f32))
    logits, mine, first = local(
        functools.partial(stats_body, 0), (*outs, shape((group, LANES), f32)), (kept, far, student, student_far)
    )
    other_logits, others, stats = local(
        functools.partial(stats_body, 1),
        (*outs, shape((block, LANES), f32)),
        (other_kept, other_far, student, student_far, first),
    )
    mask = 1
    while mask < shards:
        (stats,) = local(merge_body, (shape((block, LANES), f32),), (stats, swap(stats, "vocab", mask)))
        mask *= 2

    entries = teachers * teachers + teachers
    small, residual = local(
        residual_body,
        (shape((-(-entries // 8) * 8, LANES), f32), shape((block, width), jnp.bfloat16)),
        (logits, other_logits, mine, others, stats, labels.reshape(1, block), sib_labels.reshape(1, block)),
        scratch=[pltpu.VMEM((block, LANES), f32)],
    )
    sib_small = swap(small, "teacher", 1)
    sib_residual = swap(residual, "teacher", 1)
    far_residual = swap(residual, "teacher", 2)
    residuals = (residual, sib_residual, far_residual, swap(far_residual, "teacher", 1))
    parts = 8 if rows % 8 == 0 else 1
    squares = shape((teachers * teachers, block), f32), shape((teachers, block), f32)
    grad, cross, agree = call(
        grad_body,
        (shape((rows, width), f32), *squares),
        (turned, *residuals, small, sib_small),
        in_specs=[VMEM] * (3 + len(residuals)),
        out_specs=(any_place,) * 3,
        scratch=[
            pltpu.VMEM((parts, rows // parts, width), f32),
            pltpu.VMEM((tokens, width), residual.dtype),
            *(pltpu.VMEM(square.shape, f32) for square in squares),
            pltpu.SemaphoreType.DMA((parts + 2,)),
        ],
    )
    return cross.T.reshape(block, teachers, teachers), agree.T, grad


def normalizer(logits):
    highest = lax.pmax(jnp.max(logits, axis=1), "vocab")
    summed = lax.psum(jnp.sum(jnp.exp(logits - highest[:, None]), axis=1), "vocab")
    return highest + jnp.log(summed)


def general(teacher_hidden, teacher_head, student_hidden, student_head, labels):
    teachers = lax.axis_size("teacher")
    block_rows = student_hidden.shape[0] // teachers
    shard_width = teacher_head.shape[1]
    gathered = lax.all_gather(teacher_hidden, "vocab", axis=1, tiled=True)
    logits = jnp.dot(
        gathered[0],
        lax.all_gather(teacher_head, "teacher", axis=0, tiled=True),
        preferred_element_type=jnp.float32,
    )
    log_prob = (logits - normalizer(logits)[:, None]).astype(jnp.bfloat16)
    exchanged = lax.all_to_all(log_prob[None], "teacher", split_axis=1, concat_axis=0, tiled=True)
    teacher_prob = jnp.exp(exchanged.astype(jnp.float32)).astype(jnp.bfloat16)
    cross_local = -jnp.einsum("itv,jtv->tij", teacher_prob, exchanged, preferred_element_type=jnp.float32)
    cross_matrix = lax.psum(cross_local, "vocab")
    inverse = 1.0 / (1.0 + jnp.mean(cross_matrix, axis=1))
    weights = inverse / jnp.sum(inverse, axis=1, keepdims=True)
    soft_mix = jnp.sum(weights.T[:, :, None] * teacher_prob.astype(jnp.float32), axis=0)
    col_offset = lax.axis_index("vocab") * shard_width
    columns = lax.broadcasted_iota(jnp.int32, (block_rows, shard_width), 1) + col_offset
    onehot = (columns == labels[:, None]).astype(jnp.float32)
    target = (1.0 - HARD_SHARE) * soft_mix + HARD_SHARE * onehot
    student_logits = lax.psum_scatter(
        jnp.dot(student_hidden, student_head, preferred_element_type=jnp.float32),
        "teacher",
        scatter_dimension=0,
        tiled=True,
    )
    student_prob = jnp.exp(student_logits - normalizer(student_logits)[:, None])
    residual = (student_prob - target).astype(jnp.bfloat16)
    student_grad = lax.dot_general(
        student_hidden,
        lax.all_gather(residual, "teacher", axis=0, tiled=True),
        (((0,), (0,)), ((), ())),
        preferred_element_type=jnp.float32,
    )
    return (cross_matrix, weights * teachers, student_grad)


def solution(mesh):
    body = fast if mesh.shape["teacher"] == 4 and mesh.shape["vocab"] == 8 else general
    return jax.shard_map(
        body,
        mesh=mesh,
        in_specs=(
            P("teacher", "vocab", None),
            P("teacher", "vocab"),
            P(None, "teacher"),
            P("teacher", "vocab"),
            P("teacher"),
        ),
        out_specs=(P("teacher", None, None), P("teacher", None), P("teacher", "vocab")),
        check_vma=False,
    )
```

```python
import functools

import jax
import jax.numpy as jnp
from jax import lax
from jax.experimental import pallas as pl
from jax.experimental.pallas import tpu as pltpu
from jax.sharding import PartitionSpec as P

HARD_SHARE = 0.3
LANES = 128
TOP = 32767.0


def swap(value, axis, mask):
    count = lax.axis_size(axis)
    return lax.ppermute(value, axis, [(i, i ^ mask) for i in range(count)])


def call(body, outs, args, limit=16, scratch=(), **extra):
    return pl.pallas_call(
        body,
        out_shape=outs,
        scratch_shapes=list(scratch),
        compiler_params=pltpu.CompilerParams(vmem_limit_bytes=limit * 1024 * 1024),
        cost_estimate=pl.CostEstimate(flops=1, bytes_accessed=1, transcendentals=0),
        **extra,
    )(*args)


VMEM = pl.BlockSpec(memory_space=pltpu.VMEM)


def split_body(own_ref, far_ref, keep_ref, give_ref):
    piece, depth = keep_ref.shape[1:]
    half = depth // 2
    x = lax.axis_index("teacher") // 2
    core = lax.axis_index("teacher") % 2
    own = own_ref[...].astype(jnp.float32)
    far = far_ref[...].astype(jnp.float32)
    for at, value in enumerate((jnp.where(x == 0, own, far), jnp.where(x == 0, far, own))):
        value = jnp.where(x == 0, value[:, :depth], value[:, depth:])
        low, high = value[:piece], value[piece:]
        for ref, part, mine in (
            (keep_ref, jnp.where(core == 0, low, high), core),
            (give_ref, jnp.where(core == 0, high, low), 1 - core),
        ):
            lead, trail = part[:, :half], part[:, half:]
            ref[at, :, :half] = jnp.where(mine == 0, lead, trail).astype(ref.dtype)
            ref[at, :, half:] = jnp.where(mine == 0, trail, lead).astype(ref.dtype)


def order_body(own_ref, sib_ref, out_ref):
    core = lax.axis_index("teacher") % 2
    for i in range(own_ref.shape[0]):
        out_ref[2 * i + core] = own_ref[i]
        out_ref[2 * i + 1 - core] = sib_ref[i]


def assemble_body(*refs):
    pieces, (away_ref, stay_ref, buf) = refs[:-3], refs[-3:]
    teachers, near = away_ref.shape[:2]
    x = lax.axis_index("teacher") // 2
    level = lax.axis_index("vocab") // 2
    for mask, piece_ref in enumerate(pieces):
        buf[level ^ mask] = piece_ref[...]
    for i in range(teachers):
        for j in range(near):
            away_ref[i, j] = buf[(1 - x) * near + j, i]
            stay_ref[i, j] = buf[x * near + j, i]


def encode(value, code_ref, at):
    width = value.shape[1]
    count = jnp.floor(jnp.max(jnp.abs(value), axis=1, keepdims=True) * 0.5) + 1.0
    code = jnp.floor(value * (TOP * 0.5 / count) + 0.5)
    code_ref[(*at, slice(None), slice(0, width))] = code.astype(jnp.int32).astype(code_ref.dtype)
    count = jnp.broadcast_to(count, (value.shape[0], LANES))
    code_ref[(*at, slice(None), slice(width, width + LANES))] = count.astype(jnp.int32).astype(code_ref.dtype)


def decode(code):
    code = code.astype(jnp.int32).astype(jnp.float32)
    width = code.shape[1] - LANES
    return code[:, :width] * (code[:, width : width + 1] * (2.0 / TOP))


def partial_body(code, *refs):
    count = (len(refs) - 2 - code) // 2
    hidden_refs, (own_ref, sib_ref), out_refs = refs[:count], refs[count : count + 2], refs[count + 2 :]
    if code:
        code_ref, out_refs = out_refs[0], (out_refs[-1], *out_refs[1:-1])
    half, width = own_ref.shape
    step = min(width, 512)
    rows = [ref[...] for ref in hidden_refs]
    rows = rows[0] if count == 1 else jnp.concatenate(rows, axis=0)
    for at in range(0, width, step):
        value = jnp.dot(rows[:, :half], own_ref[:, at : at + step], preferred_element_type=jnp.float32)
        value += jnp.dot(rows[:, half:], sib_ref[:, at : at + step], preferred_element_type=jnp.float32)
        value = value.reshape(count, *out_refs[0].shape[:2], step)
        for which, out_ref in enumerate(out_refs):
            out_ref[:, :, at : at + step] = value[which]
    if code:
        for i in range(code_ref.shape[0]):
            encode(out_refs[0][i], code_ref, (i,))


def student_body(hidden_ref, head_ref, keep_ref, *refs):
    give_refs, turned_ref = refs[:-1], refs[-1]
    core = lax.axis_index("teacher") % 2
    chips, block, width = keep_ref.shape
    step = give_refs[0].shape[2]
    near = 2
    piece = block // near // 2
    tall = hidden_ref[...].astype(jnp.float32)

    def place(x, level, side, c):
        return (((x * near + level) * 2 + side) * 2 + c) * piece

    ordered = [
        tall[place(x, level, side, c) :][:piece]
        for x in range(chips)
        for c in range(2)
        for side in range(2)
        for level in range(near)
    ]
    turned_ref[...] = jnp.concatenate(ordered, axis=0).T.astype(turned_ref.dtype)
    for at, give_ref in enumerate(give_refs):
        columns = slice(at * step, (at + 1) * step)
        value = jnp.dot(hidden_ref[...], head_ref[:, columns], preferred_element_type=jnp.float32)
        for x in range(chips):
            for side in range(2):
                for level in range(near):
                    low = value[place(x, level, side, 0) :][:piece]
                    high = value[place(x, level, side, 1) :][:piece]
                    to = (side * near + level) * piece
                    keep_ref[x, to : to + piece, columns] = jnp.where(core == 0, low, high)
                    give_ref[x, to : to + piece] = jnp.where(core == 0, high, low)


def sum_body(cuts, own_ref, *refs):
    sib_refs, (keep_ref, give_ref) = refs[:cuts], refs[cuts:]
    x = lax.axis_index("teacher") // 2
    keep_ref[...] = own_ref[x] + jnp.concatenate([ref[x] for ref in sib_refs], axis=1)
    encode(own_ref[1 - x] + jnp.concatenate([ref[1 - x] for ref in sib_refs], axis=1), give_ref, ())


def stats_body(part, kept_ref, came_ref, *refs):
    if part == 0:
        student_ref, far_ref, weight_ref, student_out_ref, stats_ref, tops_ref, logits_ref = refs
    else:
        first_stats_ref, first_tops_ref, weight_ref, stats_ref, tops_ref, logits_ref = refs
    side = lax.axis_index("vocab") % 2
    teachers, rows, _ = logits_ref.shape
    lane = lax.broadcasted_iota(jnp.int32, (rows, LANES), 1)
    lse = jnp.zeros((rows, LANES), jnp.float32)
    mean = jnp.zeros((rows, LANES), jnp.float32)
    peak = jnp.zeros((rows, LANES), jnp.float32)
    tops = []
    for i in range(teachers):
        value = kept_ref[i] + decode(came_ref[i])
        tops.append(jnp.max(value, axis=1, keepdims=True))
        logits_ref[i] = value - tops[i]
    for i in range(teachers):
        weight = jnp.exp(logits_ref[i])
        weight_ref[i] = weight
        total = jnp.sum(weight, axis=1, keepdims=True)
        group = (lane >= i * teachers) & (lane < (i + 1) * teachers)
        lse = jnp.where(group, tops[i] + jnp.log(total), lse)
        peak = jnp.where(group, tops[i], peak)
        for j in range(teachers):
            local = jnp.sum(weight * logits_ref[j], axis=1, keepdims=True) / total + tops[j]
            mean = jnp.where(lane == LANES // 2 + i * teachers + j, local, mean)
    value = jnp.where(lane < LANES // 2, lse, mean)
    student_lane = lane == teachers * teachers
    own = pl.ds(pl.multiple_of(side * rows, rows), rows)
    other = pl.ds(pl.multiple_of((1 - side) * rows, rows), rows)
    if part == 0:
        student = student_ref[...] + decode(far_ref[...])
        top = jnp.max(student, axis=1, keepdims=True)
        weight = jnp.exp(student - top)
        student_out_ref[...] = weight
        wide = jnp.broadcast_to(top + jnp.log(jnp.sum(weight, axis=1, keepdims=True)), stats_ref.shape)
        stats_ref[...] = wide
        tops_ref[...] = jnp.broadcast_to(top, tops_ref.shape)
        stats_ref[own] = jnp.where(student_lane, stats_ref[own], value)
        tops_ref[own] = jnp.where(student_lane, tops_ref[own], peak)
    else:
        stats_ref[own] = first_stats_ref[own]
        tops_ref[own] = first_tops_ref[own]
        stats_ref[other] = jnp.where(student_lane, first_stats_ref[other], value)
        tops_ref[other] = jnp.where(student_lane, first_tops_ref[other], peak)


def merge_body(one_ref, two_ref, out_ref):
    half = LANES // 2
    first = lax.broadcasted_iota(jnp.int32, one_ref.shape, 1) < half
    one, two = one_ref[...], two_ref[...]
    one_lse = jnp.where(first, one, pltpu.roll(one, half, 1))
    two_lse = jnp.where(first, two, pltpu.roll(two, half, 1))
    high = jnp.maximum(one_lse, two_lse)
    both = high + jnp.log(1.0 + jnp.exp(jnp.minimum(one_lse, two_lse) - high))
    mean = jnp.exp(one_lse - both) * one + jnp.exp(two_lse - both) * two
    out_ref[...] = jnp.where(first, both, mean)


def residual_body(
    own_ref, other_ref, student_ref, tops_ref, stats_ref, label_ref, sib_label_ref, small_ref, residual_ref, weight_ref, scale_ref
):
    side = lax.axis_index("vocab") % 2
    core = lax.axis_index("teacher") % 2
    teachers, group, width = own_ref.shape
    rows = 2 * group
    lane = lax.broadcasted_iota(jnp.int32, (rows, LANES), 1)
    lse, mean = stats_ref[:, : LANES // 2], stats_ref[:, LANES // 2 :]
    small = jnp.zeros((rows, LANES), jnp.float32)
    inverse = []
    for j in range(teachers):
        norm = lse[:, j * teachers : j * teachers + 1]
        spread = jnp.zeros((rows, 1), jnp.float32)
        for i in range(teachers):
            at = i * teachers + j
            entry = norm - mean[:, at : at + 1]
            small = jnp.where(lane == at, entry, small)
            spread = spread + entry
        inverse.append(1.0 / (1.0 + spread * (1.0 / teachers)))
    total = inverse[0]
    for i in range(1, teachers):
        total = total + inverse[i]
    at = teachers * teachers
    for i in range(teachers):
        small = jnp.where(lane == at + i, inverse[i] / total * teachers, small)
    weight_ref[...] = small
    square = jnp.concatenate([small, jnp.zeros((LANES - rows, LANES), jnp.float32)], axis=0)
    small_ref[...] = square.T[: small_ref.shape[0]]
    piece = rows // 4
    token = lax.broadcasted_iota(jnp.int32, (rows, rows), 0)
    source = lax.broadcasted_iota(jnp.int32, (rows, rows), 1)
    hit = source == token // (2 * piece) * (2 * piece) + core * piece + token % piece
    mine = token // piece % 2 == core
    label = jnp.where(hit, jnp.where(mine, label_ref[...], sib_label_ref[...]), 0)
    label = jnp.sum(label, axis=1, keepdims=True) - lax.axis_index("vocab") * width
    label_at = lambda place: jnp.where(place == 0, label[:group], label[group:])
    scale = jnp.where(lane <= at, jnp.exp(jnp.minimum(tops_ref[...] - stats_ref[...], 0.0)), 0.0)
    scale_ref[...] = scale
    for part, exp_ref in enumerate((own_ref, other_ref)):
        place = side if part == 0 else 1 - side
        span = pl.ds(pl.multiple_of(place * group, group), group)
        scales = scale_ref[span]
        weights = weight_ref[span]
        target = jnp.where(
            lax.broadcasted_iota(jnp.int32, (group, width), 1) == label_at(place), HARD_SHARE, 0.0
        )
        for i in range(teachers):
            share = (1.0 - HARD_SHARE) / teachers * weights[:, at + i : at + i + 1]
            target = target + share * scales[:, i * teachers : i * teachers + 1] * exp_ref[i]
        prob = student_ref[span] * scales[:, at : at + 1]
        residual_ref[span] = (prob - target).astype(jnp.bfloat16)


def grad_body(hidden_ref, *refs):
    count = lax.axis_size("teacher")
    residual_refs, (small_ref, sib_ref, grad_ref, cross_ref, agree_ref) = refs[:-10], refs[-10:-5]
    buf, rows_ref, cross_buf, agree_buf, sems = refs[-5:]
    if len(residual_refs) > 1:
        me = lax.axis_index("teacher")
        size = rows_ref.shape[0] // count
        for mask, ref in enumerate(residual_refs):
            rows_ref[pl.ds(pl.multiple_of((me ^ mask) * size, size), size)] = ref[...]
    else:
        rows_ref = residual_refs[0]
    parts, step, _ = buf.shape
    copies = []

    def send(value, ref):
        copies.append(pltpu.make_async_copy(value, ref, sems.at[len(copies)]))
        copies[-1].start()

    for at in range(parts):
        rows = pl.ds(at * step, step)
        buf[at] = jnp.dot(hidden_ref[rows], rows_ref[...], preferred_element_type=jnp.float32)
        send(buf.at[at], grad_ref.at[rows])
        if at == 0:
            core = lax.axis_index("teacher") % 2
            block = cross_buf.shape[1]
            piece = block // 4
            source = lax.broadcasted_iota(jnp.int32, (LANES, block), 0)
            token = lax.broadcasted_iota(jnp.int32, (LANES, block), 1)
            hit = source == token // (2 * piece) * (2 * piece) + core * piece + token % piece
            mine = token // piece % 2 == core
            placed = sum(
                jnp.dot(
                    ref[...],
                    jnp.where(hit & which, 1.0, 0.0),
                    preferred_element_type=jnp.float32,
                    precision=lax.Precision.HIGHEST,
                )
                for ref, which in ((small_ref, mine), (sib_ref, jnp.logical_not(mine)))
            )
            entries = cross_buf.shape[0]
            cross_buf[...] = placed[:entries]
            agree_buf[...] = placed[entries : entries + agree_buf.shape[0]]
            send(cross_buf, cross_ref)
            send(agree_buf, agree_ref)
    for copy in copies:
        copy.wait()


def fast(teacher_hidden, teacher_head, student_hidden, student_head, labels):
    teachers = lax.axis_size("teacher")
    shards = lax.axis_size("vocab")
    chips = teachers // 2
    rows, width = teacher_head.shape
    tokens = student_hidden.shape[0]
    near = shards // 2 // chips
    piece = tokens // shards // 2
    block = tokens // teachers
    group = block // 2
    f32 = jnp.float32
    kind = teacher_hidden.dtype
    shape = jax.ShapeDtypeStruct

    any_place = pl.BlockSpec(memory_space=pl.ANY)

    def local(body, outs, args, after=(), specs=None, **extra):
        specs = [VMEM] * len(args) if specs is None else specs
        skip = len(after)
        return call(
            (lambda *refs: body(*refs[skip:])) if after else body,
            outs,
            (*after, *args),
            in_specs=[any_place] * skip + specs,
            out_specs=(VMEM,) * len(outs),
            **extra,
        )

    own = teacher_hidden[0]
    far = swap(own, "teacher", 2)
    keep, give = local(split_body, (shape((2, piece, 2 * rows), kind),) * 2, (own, far))
    split = keep
    (part,) = local(order_body, (shape((teachers, piece, 2 * rows), kind),), (keep, swap(give, "teacher", 1)))
    parts = [part] + [swap(part, "vocab", 2 * mask) for mask in range(1, shards // 2)]
    sib_head = swap(teacher_head, "teacher", 1)
    sib_labels = swap(labels, "teacher", 1)
    cuts = max(1, min(4, width // LANES))
    mine, *others, turned = local(
        student_body,
        (
            shape((chips, block, width), f32),
            *(shape((chips, block, width // cuts), f32),) * cuts,
            shape((rows, tokens), student_hidden.dtype),
        ),
        (student_hidden, student_head),
        after=(),
    )
    others = [swap(value, "teacher", 1) for value in others]
    coded = functools.partial(shape, dtype=jnp.int16)
    student, give = local(
        functools.partial(sum_body, cuts),
        (shape((block, width), f32), coded((block, width + LANES))),
        (mine, *others),
        after=(sib_head,),
    )
    student_far = swap(give, "teacher", 2)
    away, stay = local(
        assemble_body,
        (shape((teachers, near, piece, 2 * rows), kind),) * 2,
        parts,
        scratch=[pltpu.VMEM((shards // 2, teachers, piece, 2 * rows), kind)],
    )
    away = away.reshape(teachers * group, 2 * rows)
    stay = stay.reshape(teachers * group, 2 * rows)

    flat = shape((teachers, group, width), f32)

    def partial(outs, *hidden):
        code = outs[0].dtype == jnp.int16
        return local(
            functools.partial(partial_body, int(code)),
            outs,
            (*hidden, teacher_head, sib_head),
            scratch=[pltpu.VMEM(flat.shape, f32)] if code else (),
        )

    code = coded((teachers, group, width + LANES))
    sent, kept = partial((code, flat), away, stay)
    sent, away, stay = lax.optimization_barrier((sent, away, stay))
    far = swap(sent, "teacher", 2)
    other_away = swap(away, "vocab", 1)
    stay, far = lax.optimization_barrier((stay, far))
    other_away, student_far = lax.optimization_barrier((other_away, student_far))
    other_stay = swap(stay, "vocab", 1)
    (other_sent,) = partial((code,), other_away)
    other_far = swap(other_sent, "teacher", 2)
    (other_kept,) = partial((flat,), other_stay)

    lists = (shape((block, LANES), f32),) * 2
    scratch = [pltpu.VMEM(flat.shape, f32)]
    weights, student_weights, *firsts = local(
        functools.partial(stats_body, 0),
        (flat, shape((block, width), f32), *lists),
        (kept, far, student, student_far),
        scratch=scratch,
    )
    other_weights, stats, tops = local(
        functools.partial(stats_body, 1), (flat, *lists), (other_kept, other_far, *firsts), scratch=scratch
    )
    mask = 1
    while mask < shards:
        (stats,) = local(merge_body, (shape((block, LANES), f32),), (stats, swap(stats, "vocab", mask)))
        mask *= 2

    entries = teachers * teachers + teachers
    small, residual = local(
        residual_body,
        (shape((-(-entries // 8) * 8, LANES), f32), shape((block, width), jnp.bfloat16)),
        (weights, other_weights, student_weights, tops, stats, labels.reshape(1, block), sib_labels.reshape(1, block)),
        scratch=[pltpu.VMEM((block, LANES), f32)] * 2,
    )
    sib_small = swap(small, "teacher", 1)
    sib_residual = swap(residual, "teacher", 1)
    far_residual = swap(residual, "teacher", 2)
    residuals = (residual, sib_residual, far_residual, swap(far_residual, "teacher", 1))
    parts = 8 if rows % 8 == 0 else 1
    squares = shape((teachers * teachers, block), f32), shape((teachers, block), f32)
    grad, cross, agree = call(
        grad_body,
        (shape((rows, width), f32), *squares),
        (turned, *residuals, small, sib_small),
        in_specs=[VMEM] * (3 + len(residuals)),
        out_specs=(any_place,) * 3,
        scratch=[
            pltpu.VMEM((parts, rows // parts, width), f32),
            pltpu.VMEM((tokens, width), residual.dtype),
            *(pltpu.VMEM(square.shape, f32) for square in squares),
            pltpu.SemaphoreType.DMA((parts + 2,)),
        ],
    )
    return cross.T.reshape(block, teachers, teachers), agree.T, grad


def normalizer(logits):
    highest = lax.pmax(jnp.max(logits, axis=1), "vocab")
    summed = lax.psum(jnp.sum(jnp.exp(logits - highest[:, None]), axis=1), "vocab")
    return highest + jnp.log(summed)


def general(teacher_hidden, teacher_head, student_hidden, student_head, labels):
    teachers = lax.axis_size("teacher")
    block_rows = student_hidden.shape[0] // teachers
    shard_width = teacher_head.shape[1]
    gathered = lax.all_gather(teacher_hidden, "vocab", axis=1, tiled=True)
    logits = jnp.dot(
        gathered[0],
        lax.all_gather(teacher_head, "teacher", axis=0, tiled=True),
        preferred_element_type=jnp.float32,
    )
    log_prob = (logits - normalizer(logits)[:, None]).astype(jnp.bfloat16)
    exchanged = lax.all_to_all(log_prob[None], "teacher", split_axis=1, concat_axis=0, tiled=True)
    teacher_prob = jnp.exp(exchanged.astype(jnp.float32)).astype(jnp.bfloat16)
    cross_local = -jnp.einsum("itv,jtv->tij", teacher_prob, exchanged, preferred_element_type=jnp.float32)
    cross_matrix = lax.psum(cross_local, "vocab")
    inverse = 1.0 / (1.0 + jnp.mean(cross_matrix, axis=1))
    weights = inverse / jnp.sum(inverse, axis=1, keepdims=True)
    soft_mix = jnp.sum(weights.T[:, :, None] * teacher_prob.astype(jnp.float32), axis=0)
    col_offset = lax.axis_index("vocab") * shard_width
    columns = lax.broadcasted_iota(jnp.int32, (block_rows, shard_width), 1) + col_offset
    onehot = (columns == labels[:, None]).astype(jnp.float32)
    target = (1.0 - HARD_SHARE) * soft_mix + HARD_SHARE * onehot
    student_logits = lax.psum_scatter(
        jnp.dot(student_hidden, student_head, preferred_element_type=jnp.float32),
        "teacher",
        scatter_dimension=0,
        tiled=True,
    )
    student_prob = jnp.exp(student_logits - normalizer(student_logits)[:, None])
    residual = (student_prob - target).astype(jnp.bfloat16)
    student_grad = lax.dot_general(
        student_hidden,
        lax.all_gather(residual, "teacher", axis=0, tiled=True),
        (((0,), (0,)), ((), ())),
        preferred_element_type=jnp.float32,
    )
    return (cross_matrix, weights * teachers, student_grad)


def solution(mesh):
    body = fast if mesh.shape["teacher"] == 4 and mesh.shape["vocab"] == 8 else general
    return jax.shard_map(
        body,
        mesh=mesh,
        in_specs=(
            P("teacher", "vocab", None),
            P("teacher", "vocab"),
            P(None, "teacher"),
            P("teacher", "vocab"),
            P("teacher"),
        ),
        out_specs=(P("teacher", None, None), P("teacher", None), P("teacher", "vocab")),
        check_vma=False,
    )
```

```python
import functools

import jax
import jax.numpy as jnp
from jax import lax
from jax.experimental import pallas as pl
from jax.experimental.pallas import tpu as pltpu
from jax.sharding import PartitionSpec as P

HARD_SHARE = 0.3
LANES = 128
TOP = 32767.0


def swap(value, axis, mask):
    count = lax.axis_size(axis)
    return lax.ppermute(value, axis, [(i, i ^ mask) for i in range(count)])


def call(body, outs, args, limit=16, scratch=(), **extra):
    return pl.pallas_call(
        body,
        out_shape=outs,
        scratch_shapes=list(scratch),
        compiler_params=pltpu.CompilerParams(vmem_limit_bytes=limit * 1024 * 1024),
        cost_estimate=pl.CostEstimate(flops=1, bytes_accessed=1, transcendentals=0),
        **extra,
    )(*args)


VMEM = pl.BlockSpec(memory_space=pltpu.VMEM)


def split_body(own_ref, far_ref, keep_ref, give_ref):
    piece, depth = keep_ref.shape[1:]
    half = depth // 2
    x = lax.axis_index("teacher") // 2
    core = lax.axis_index("teacher") % 2
    own = own_ref[...].astype(jnp.float32)
    far = far_ref[...].astype(jnp.float32)
    for at, value in enumerate((jnp.where(x == 0, own, far), jnp.where(x == 0, far, own))):
        value = jnp.where(x == 0, value[:, :depth], value[:, depth:])
        low, high = value[:piece], value[piece:]
        for ref, part, mine in (
            (keep_ref, jnp.where(core == 0, low, high), core),
            (give_ref, jnp.where(core == 0, high, low), 1 - core),
        ):
            lead, trail = part[:, :half], part[:, half:]
            ref[at, :, :half] = jnp.where(mine == 0, lead, trail).astype(ref.dtype)
            ref[at, :, half:] = jnp.where(mine == 0, trail, lead).astype(ref.dtype)


def order_body(own_ref, sib_ref, out_ref):
    core = lax.axis_index("teacher") % 2
    for i in range(own_ref.shape[0]):
        out_ref[2 * i + core] = own_ref[i]
        out_ref[2 * i + 1 - core] = sib_ref[i]


def assemble_body(*refs):
    pieces, (away_ref, stay_ref, buf) = refs[:-3], refs[-3:]
    teachers, near = away_ref.shape[:2]
    x = lax.axis_index("teacher") // 2
    level = lax.axis_index("vocab") // 2
    for mask, piece_ref in enumerate(pieces):
        buf[level ^ mask] = piece_ref[...]
    for i in range(teachers):
        for j in range(near):
            away_ref[i, j] = buf[(1 - x) * near + j, i]
            stay_ref[i, j] = buf[x * near + j, i]


def encode(value, code_ref, at):
    width = value.shape[1]
    count = jnp.floor(jnp.max(jnp.abs(value), axis=1, keepdims=True) * 0.5) + 1.0
    code = jnp.floor(value * (TOP * 0.5 / count) + 0.5)
    code_ref[(*at, slice(None), slice(0, width))] = code.astype(jnp.int32).astype(code_ref.dtype)
    count = jnp.broadcast_to(count, (value.shape[0], LANES))
    code_ref[(*at, slice(None), slice(width, width + LANES))] = count.astype(jnp.int32).astype(code_ref.dtype)


def decode(code):
    code = code.astype(jnp.int32).astype(jnp.float32)
    width = code.shape[1] - LANES
    return code[:, :width] * (code[:, width : width + 1] * (2.0 / TOP))


def partial_body(code, *refs):
    count = (len(refs) - 2 - code) // 2
    hidden_refs, (own_ref, sib_ref), out_refs = refs[:count], refs[count : count + 2], refs[count + 2 :]
    if code:
        code_ref, out_refs = out_refs[0], (out_refs[-1], *out_refs[1:-1])
    half, width = own_ref.shape
    step = min(width, 512)
    rows = [ref[...] for ref in hidden_refs]
    rows = rows[0] if count == 1 else jnp.concatenate(rows, axis=0)
    for at in range(0, width, step):
        value = jnp.dot(rows[:, :half], own_ref[:, at : at + step], preferred_element_type=jnp.float32)
        value += jnp.dot(rows[:, half:], sib_ref[:, at : at + step], preferred_element_type=jnp.float32)
        value = value.reshape(count, *out_refs[0].shape[:2], step)
        for which, out_ref in enumerate(out_refs):
            out_ref[:, :, at : at + step] = value[which]
    if code:
        for i in range(code_ref.shape[0]):
            encode(out_refs[0][i], code_ref, (i,))


def student_body(hidden_ref, head_ref, keep_ref, *refs):
    give_refs, turned_ref = refs[:-1], refs[-1]
    core = lax.axis_index("teacher") % 2
    chips, block, width = keep_ref.shape
    step = give_refs[0].shape[2]
    near = 2
    piece = block // near // 2
    tall = hidden_ref[...].astype(jnp.float32)

    def place(x, level, side, c):
        return (((x * near + level) * 2 + side) * 2 + c) * piece

    ordered = [
        tall[place(x, level, side, c) :][:piece]
        for x in range(chips)
        for c in range(2)
        for side in range(2)
        for level in range(near)
    ]
    turned_ref[...] = jnp.concatenate(ordered, axis=0).T.astype(turned_ref.dtype)
    for at, give_ref in enumerate(give_refs):
        columns = slice(at * step, (at + 1) * step)
        value = jnp.dot(hidden_ref[...], head_ref[:, columns], preferred_element_type=jnp.float32)
        for x in range(chips):
            for side in range(2):
                for level in range(near):
                    low = value[place(x, level, side, 0) :][:piece]
                    high = value[place(x, level, side, 1) :][:piece]
                    to = (side * near + level) * piece
                    keep_ref[x, to : to + piece, columns] = jnp.where(core == 0, low, high)
                    give_ref[x, to : to + piece] = jnp.where(core == 0, high, low)


def sum_body(cuts, own_ref, *refs):
    sib_refs, (keep_ref, give_ref) = refs[:cuts], refs[cuts:]
    x = lax.axis_index("teacher") // 2
    keep_ref[...] = own_ref[x] + jnp.concatenate([ref[x] for ref in sib_refs], axis=1)
    encode(own_ref[1 - x] + jnp.concatenate([ref[1 - x] for ref in sib_refs], axis=1), give_ref, ())


def stats_body(part, kept_ref, came_ref, *refs):
    if part == 0:
        student_ref, far_ref, weight_ref, student_out_ref, stats_ref, tops_ref, logits_ref = refs
    else:
        first_stats_ref, first_tops_ref, weight_ref, stats_ref, tops_ref, logits_ref = refs
    side = lax.axis_index("vocab") % 2
    teachers, rows, _ = logits_ref.shape
    lane = lax.broadcasted_iota(jnp.int32, (rows, LANES), 1)
    lse = jnp.zeros((rows, LANES), jnp.float32)
    mean = jnp.zeros((rows, LANES), jnp.float32)
    peak = jnp.zeros((rows, LANES), jnp.float32)
    tops = []
    for i in range(teachers):
        value = kept_ref[i] + decode(came_ref[i])
        tops.append(jnp.max(value, axis=1, keepdims=True))
        logits_ref[i] = value - tops[i]
    for i in range(teachers):
        weight = jnp.exp(logits_ref[i])
        weight_ref[i] = weight
        total = jnp.sum(weight, axis=1, keepdims=True)
        group = (lane >= i * teachers) & (lane < (i + 1) * teachers)
        lse = jnp.where(group, tops[i] + jnp.log(total), lse)
        peak = jnp.where(group, tops[i], peak)
        for j in range(teachers):
            local = jnp.sum(weight * logits_ref[j], axis=1, keepdims=True) / total + tops[j]
            mean = jnp.where(lane == LANES // 2 + i * teachers + j, local, mean)
    value = jnp.where(lane < LANES // 2, lse, mean)
    student_lane = lane == teachers * teachers
    own = pl.ds(pl.multiple_of(side * rows, rows), rows)
    other = pl.ds(pl.multiple_of((1 - side) * rows, rows), rows)
    if part == 0:
        student = student_ref[...] + decode(far_ref[...])
        top = jnp.max(student, axis=1, keepdims=True)
        weight = jnp.exp(student - top)
        student_out_ref[...] = weight
        wide = jnp.broadcast_to(top + jnp.log(jnp.sum(weight, axis=1, keepdims=True)), stats_ref.shape)
        stats_ref[...] = wide
        tops_ref[...] = jnp.broadcast_to(top, tops_ref.shape)
        stats_ref[own] = jnp.where(student_lane, stats_ref[own], value)
        tops_ref[own] = jnp.where(student_lane, tops_ref[own], peak)
    else:
        stats_ref[own] = first_stats_ref[own]
        tops_ref[own] = first_tops_ref[own]
        stats_ref[other] = jnp.where(student_lane, first_stats_ref[other], value)
        tops_ref[other] = jnp.where(student_lane, first_tops_ref[other], peak)


def merge_body(one_ref, two_ref, out_ref):
    half = LANES // 2
    first = lax.broadcasted_iota(jnp.int32, one_ref.shape, 1) < half
    one, two = one_ref[...], two_ref[...]
    one_lse = jnp.where(first, one, pltpu.roll(one, half, 1))
    two_lse = jnp.where(first, two, pltpu.roll(two, half, 1))
    high = jnp.maximum(one_lse, two_lse)
    both = high + jnp.log(1.0 + jnp.exp(jnp.minimum(one_lse, two_lse) - high))
    mean = jnp.exp(one_lse - both) * one + jnp.exp(two_lse - both) * two
    out_ref[...] = jnp.where(first, both, mean)


def residual_body(
    own_ref, other_ref, student_ref, tops_ref, stats_ref, label_ref, sib_label_ref, small_ref, residual_ref, weight_ref, scale_ref
):
    side = lax.axis_index("vocab") % 2
    core = lax.axis_index("teacher") % 2
    teachers, group, width = own_ref.shape
    rows = 2 * group
    lane = lax.broadcasted_iota(jnp.int32, (rows, LANES), 1)
    lse, mean = stats_ref[:, : LANES // 2], stats_ref[:, LANES // 2 :]
    small = jnp.zeros((rows, LANES), jnp.float32)
    inverse = []
    for j in range(teachers):
        norm = lse[:, j * teachers : j * teachers + 1]
        spread = jnp.zeros((rows, 1), jnp.float32)
        for i in range(teachers):
            at = i * teachers + j
            entry = norm - mean[:, at : at + 1]
            small = jnp.where(lane == at, entry, small)
            spread = spread + entry
        inverse.append(1.0 / (1.0 + spread * (1.0 / teachers)))
    total = inverse[0]
    for i in range(1, teachers):
        total = total + inverse[i]
    at = teachers * teachers
    for i in range(teachers):
        small = jnp.where(lane == at + i, inverse[i] / total * teachers, small)
    weight_ref[...] = small
    square = jnp.concatenate([small, jnp.zeros((LANES - rows, LANES), jnp.float32)], axis=0)
    small_ref[...] = square.T[: small_ref.shape[0]]
    piece = rows // 4
    token = lax.broadcasted_iota(jnp.int32, (rows, rows), 0)
    source = lax.broadcasted_iota(jnp.int32, (rows, rows), 1)
    hit = source == token // (2 * piece) * (2 * piece) + core * piece + token % piece
    mine = token // piece % 2 == core
    label = jnp.where(hit, jnp.where(mine, label_ref[...], sib_label_ref[...]), 0)
    label = jnp.sum(label, axis=1, keepdims=True) - lax.axis_index("vocab") * width
    label_at = lambda place: jnp.where(place == 0, label[:group], label[group:])
    scale = jnp.where(lane <= at, jnp.exp(jnp.minimum(tops_ref[...] - stats_ref[...], 0.0)), 0.0)
    scale_ref[...] = scale
    for part, exp_ref in enumerate((own_ref, other_ref)):
        place = side if part == 0 else 1 - side
        span = pl.ds(pl.multiple_of(place * group, group), group)
        scales = scale_ref[span]
        weights = weight_ref[span]
        target = jnp.where(
            lax.broadcasted_iota(jnp.int32, (group, width), 1) == label_at(place), HARD_SHARE, 0.0
        )
        for i in range(teachers):
            share = (1.0 - HARD_SHARE) / teachers * weights[:, at + i : at + i + 1]
            target = target + share * scales[:, i * teachers : i * teachers + 1] * exp_ref[i]
        prob = student_ref[span] * scales[:, at : at + 1]
        residual_ref[span] = (prob - target).astype(jnp.bfloat16)


def grad_body(hidden_ref, *refs):
    count = lax.axis_size("teacher")
    residual_refs, (small_ref, sib_ref, grad_ref, cross_ref, agree_ref) = refs[:-10], refs[-10:-5]
    buf, rows_ref, cross_buf, agree_buf, sems = refs[-5:]
    if len(residual_refs) > 1:
        me = lax.axis_index("teacher")
        size = rows_ref.shape[0] // count
        for mask, ref in enumerate(residual_refs):
            rows_ref[pl.ds(pl.multiple_of((me ^ mask) * size, size), size)] = ref[...]
    else:
        rows_ref = residual_refs[0]
    parts, step, _ = buf.shape
    copies = []

    def send(value, ref):
        copies.append(pltpu.make_async_copy(value, ref, sems.at[len(copies)]))
        copies[-1].start()

    for at in range(parts):
        rows = pl.ds(at * step, step)
        buf[at] = jnp.dot(hidden_ref[rows], rows_ref[...], preferred_element_type=jnp.float32)
        send(buf.at[at], grad_ref.at[rows])
        if at == 0:
            core = lax.axis_index("teacher") % 2
            block = cross_buf.shape[1]
            piece = block // 4
            source = lax.broadcasted_iota(jnp.int32, (LANES, block), 0)
            token = lax.broadcasted_iota(jnp.int32, (LANES, block), 1)
            hit = source == token // (2 * piece) * (2 * piece) + core * piece + token % piece
            mine = token // piece % 2 == core
            placed = sum(
                jnp.dot(
                    ref[...],
                    jnp.where(hit & which, 1.0, 0.0),
                    preferred_element_type=jnp.float32,
                    precision=lax.Precision.HIGHEST,
                )
                for ref, which in ((small_ref, mine), (sib_ref, jnp.logical_not(mine)))
            )
            entries = cross_buf.shape[0]
            cross_buf[...] = placed[:entries]
            agree_buf[...] = placed[entries : entries + agree_buf.shape[0]]
            send(cross_buf, cross_ref)
            send(agree_buf, agree_ref)
    for copy in copies:
        copy.wait()


def fast(teacher_hidden, teacher_head, student_hidden, student_head, labels):
    teachers = lax.axis_size("teacher")
    shards = lax.axis_size("vocab")
    chips = teachers // 2
    rows, width = teacher_head.shape
    tokens = student_hidden.shape[0]
    near = shards // 2 // chips
    piece = tokens // shards // 2
    block = tokens // teachers
    group = block // 2
    f32 = jnp.float32
    kind = teacher_hidden.dtype
    shape = jax.ShapeDtypeStruct

    any_place = pl.BlockSpec(memory_space=pl.ANY)

    def local(body, outs, args, after=(), specs=None, **extra):
        specs = [VMEM] * len(args) if specs is None else specs
        skip = len(after)
        return call(
            (lambda *refs: body(*refs[skip:])) if after else body,
            outs,
            (*after, *args),
            in_specs=[any_place] * skip + specs,
            out_specs=(VMEM,) * len(outs),
            **extra,
        )

    own = teacher_hidden[0]
    far = swap(own, "teacher", 2)
    keep, give = local(split_body, (shape((2, piece, 2 * rows), kind),) * 2, (own, far))
    split = keep
    (part,) = local(order_body, (shape((teachers, piece, 2 * rows), kind),), (keep, swap(give, "teacher", 1)))
    parts = [part] + [swap(part, "vocab", 2 * mask) for mask in range(1, shards // 2)]
    sib_head = swap(teacher_head, "teacher", 1)
    sib_labels = swap(labels, "teacher", 1)
    cuts = max(1, min(4, width // LANES))
    mine, *others, turned = local(
        student_body,
        (
            shape((chips, block, width), f32),
            *(shape((chips, block, width // cuts), f32),) * cuts,
            shape((rows, tokens), student_hidden.dtype),
        ),
        (student_hidden, student_head),
        after=(),
    )
    others = [swap(value, "teacher", 1) for value in others]
    coded = functools.partial(shape, dtype=jnp.int16)
    student, give = local(
        functools.partial(sum_body, cuts),
        (shape((block, width), f32), coded((block, width + LANES))),
        (mine, *others),
        after=(part,),
    )
    student_far = swap(give, "teacher", 2)
    away, stay = local(
        assemble_body,
        (shape((teachers, near, piece, 2 * rows), kind),) * 2,
        parts,
        scratch=[pltpu.VMEM((shards // 2, teachers, piece, 2 * rows), kind)],
    )
    away = away.reshape(teachers * group, 2 * rows)
    stay = stay.reshape(teachers * group, 2 * rows)

    flat = shape((teachers, group, width), f32)

    def partial(outs, *hidden):
        code = outs[0].dtype == jnp.int16
        return local(
            functools.partial(partial_body, int(code)),
            outs,
            (*hidden, teacher_head, sib_head),
            scratch=[pltpu.VMEM(flat.shape, f32)] if code else (),
        )

    code = coded((teachers, group, width + LANES))
    sent, kept = partial((code, flat), away, stay)
    sent, away, stay = lax.optimization_barrier((sent, away, stay))
    far = swap(sent, "teacher", 2)
    other_away = swap(away, "vocab", 1)
    stay, far = lax.optimization_barrier((stay, far))
    other_away, student_far = lax.optimization_barrier((other_away, student_far))
    other_stay = swap(stay, "vocab", 1)
    (other_sent,) = partial((code,), other_away)
    other_far = swap(other_sent, "teacher", 2)
    (other_kept,) = partial((flat,), other_stay)

    lists = (shape((block, LANES), f32),) * 2
    scratch = [pltpu.VMEM(flat.shape, f32)]
    weights, student_weights, *firsts = local(
        functools.partial(stats_body, 0),
        (flat, shape((block, width), f32), *lists),
        (kept, far, student, student_far),
        scratch=scratch,
    )
    other_weights, stats, tops = local(
        functools.partial(stats_body, 1), (flat, *lists), (other_kept, other_far, *firsts), scratch=scratch
    )
    mask = 1
    while mask < shards:
        (stats,) = local(merge_body, (shape((block, LANES), f32),), (stats, swap(stats, "vocab", mask)))
        mask *= 2

    entries = teachers * teachers + teachers
    small, residual = local(
        residual_body,
        (shape((-(-entries // 8) * 8, LANES), f32), shape((block, width), jnp.bfloat16)),
        (weights, other_weights, student_weights, tops, stats, labels.reshape(1, block), sib_labels.reshape(1, block)),
        scratch=[pltpu.VMEM((block, LANES), f32)] * 2,
    )
    sib_small = swap(small, "teacher", 1)
    sib_residual = swap(residual, "teacher", 1)
    far_residual = swap(residual, "teacher", 2)
    residuals = (residual, sib_residual, far_residual, swap(far_residual, "teacher", 1))
    parts = 8 if rows % 8 == 0 else 1
    squares = shape((teachers * teachers, block), f32), shape((teachers, block), f32)
    grad, cross, agree = call(
        grad_body,
        (shape((rows, width), f32), *squares),
        (turned, *residuals, small, sib_small),
        in_specs=[VMEM] * (3 + len(residuals)),
        out_specs=(any_place,) * 3,
        scratch=[
            pltpu.VMEM((parts, rows // parts, width), f32),
            pltpu.VMEM((tokens, width), residual.dtype),
            *(pltpu.VMEM(square.shape, f32) for square in squares),
            pltpu.SemaphoreType.DMA((parts + 2,)),
        ],
    )
    return cross.T.reshape(block, teachers, teachers), agree.T, grad


def normalizer(logits):
    highest = lax.pmax(jnp.max(logits, axis=1), "vocab")
    summed = lax.psum(jnp.sum(jnp.exp(logits - highest[:, None]), axis=1), "vocab")
    return highest + jnp.log(summed)


def general(teacher_hidden, teacher_head, student_hidden, student_head, labels):
    teachers = lax.axis_size("teacher")
    block_rows = student_hidden.shape[0] // teachers
    shard_width = teacher_head.shape[1]
    gathered = lax.all_gather(teacher_hidden, "vocab", axis=1, tiled=True)
    logits = jnp.dot(
        gathered[0],
        lax.all_gather(teacher_head, "teacher", axis=0, tiled=True),
        preferred_element_type=jnp.float32,
    )
    log_prob = (logits - normalizer(logits)[:, None]).astype(jnp.bfloat16)
    exchanged = lax.all_to_all(log_prob[None], "teacher", split_axis=1, concat_axis=0, tiled=True)
    teacher_prob = jnp.exp(exchanged.astype(jnp.float32)).astype(jnp.bfloat16)
    cross_local = -jnp.einsum("itv,jtv->tij", teacher_prob, exchanged, preferred_element_type=jnp.float32)
    cross_matrix = lax.psum(cross_local, "vocab")
    inverse = 1.0 / (1.0 + jnp.mean(cross_matrix, axis=1))
    weights = inverse / jnp.sum(inverse, axis=1, keepdims=True)
    soft_mix = jnp.sum(weights.T[:, :, None] * teacher_prob.astype(jnp.float32), axis=0)
    col_offset = lax.axis_index("vocab") * shard_width
    columns = lax.broadcasted_iota(jnp.int32, (block_rows, shard_width), 1) + col_offset
    onehot = (columns == labels[:, None]).astype(jnp.float32)
    target = (1.0 - HARD_SHARE) * soft_mix + HARD_SHARE * onehot
    student_logits = lax.psum_scatter(
        jnp.dot(student_hidden, student_head, preferred_element_type=jnp.float32),
        "teacher",
        scatter_dimension=0,
        tiled=True,
    )
    student_prob = jnp.exp(student_logits - normalizer(student_logits)[:, None])
    residual = (student_prob - target).astype(jnp.bfloat16)
    student_grad = lax.dot_general(
        student_hidden,
        lax.all_gather(residual, "teacher", axis=0, tiled=True),
        (((0,), (0,)), ((), ())),
        preferred_element_type=jnp.float32,
    )
    return (cross_matrix, weights * teachers, student_grad)


def solution(mesh):
    body = fast if mesh.shape["teacher"] == 4 and mesh.shape["vocab"] == 8 else general
    return jax.shard_map(
        body,
        mesh=mesh,
        in_specs=(
            P("teacher", "vocab", None),
            P("teacher", "vocab"),
            P(None, "teacher"),
            P("teacher", "vocab"),
            P("teacher"),
        ),
        out_specs=(P("teacher", None, None), P("teacher", None), P("teacher", "vocab")),
        check_vma=False,
    )
```
